256 devices in a mesh: req: 32 (over z, y), tp: 8 (over x, core).
Axes of the slice: x: 4, y: 4, z: 8, core: 2. Of those that a mesh axis runs over, the one named last changes fastest.
Arguments:
- ssm_input: bfloat16 [32, 512, 8192], P('req', 'tp'), may hold values from -6 to 6
- ssm_gate: bfloat16 [32, 512, 8192], P('req', 'tp'), may hold values from -6 to 6
- state_proj: bfloat16 [32, 512, 4096], P('req', 'tp'), may hold values from -1.796875 to 1.796875
- step_raw: bfloat16 [32, 512, 128], P('req', 'tp'), may hold values from -3 to 3
- queries: bfloat16 [32, 512, 4096], P('req', 'tp'), may hold values from -5 to 5
- fresh_kv: bfloat16 [32, 512, 2048], P('req', 'tp'), may hold values from -6 to 6
- block_pool: bfloat16 [128, 64, 8, 256], P('req', None, 'tp'), may hold values from -5 to 5
- state_pool: bfloat16 [32, 128, 64, 256], P('req', 'tp'), may hold values from -16 to 16
- decay_log: float32 [128], P('tp'), may hold values from -10 to -1
- step_bias: float32 [128], P('tp'), may hold values from -1 to 0
- skip_gain: float32 [128], P('tp'), may hold values from 1 to 3
- norm_gain: float32 [8192], P('tp'), may hold values from 0.5 to 1.5
- block_owner: int32 [32, 64], replicated, may hold values from 0 to 31, as said below
- block_slot: int32 [32, 64], replicated, may hold values from 0 to 3, as said below
- block_count: int32 [32], replicated, may hold values from 32 to 64, as said below
- state_entry: int32 [32], replicated, may hold values from 0 to 31
- suffix_len: int32 [32], replicated, may hold values from 128 to 512, as said below
Outputs:
- ssm_out: bfloat16 [32, 512, 8192], P('req', 'tp')
- attn_out: bfloat16 [32, 512, 4096], P('req', 'tp')
The draws below stay inside these ranges and needn't reach their ends.
Inputs may be any that keep to these rules, and one draw needn't show every extreme that they name: `block_owner`: among the first block_count[r] entries of a request no owner appears more than 2 times; in every draw one request has 64 entries in use and takes exactly 2 from every owner. The owner at entry j is named again at entry j + 32. Requests 4k to 4k + 3 name the same owners at every entry. `block_slot`: requests 4k to 4k + 3 name the same blocks in their first 32 entries. `block_count`: some request has 64 in every draw. `suffix_len`: some request has 512 in every draw.
All inputs are finite; a program needn't handle non-finite values.
Results may differ from the reference program's by a relative error of at most 0.0048.
Values may be sent and summed in bfloat16 or wider, within the bound.
A program may use at most 128 MiB of HBM per device.

```python
import jax
import jax.numpy as jnp
from jax import lax

MHEADS = 128
HEAD_DIM = 64
STATE = 256
GROUPS = 8
QHEADS = 32
KVHEADS = 8
ATT_DIM = 128
SPAN = 256
BLOCK = 64
SUFFIX = 512
MAXBLK = 64
POOL_DEV = 4
REQS = 32
ENTRIES = 32
POOL = 128


def block_tables(key):
    key = jax.random.fold_in(key, 5)
    key_perm, key_shared, key_own = jax.random.split(key, 3)
    group_total = (REQS + 3) // 4
    perm_keys = jax.random.split(key_perm, group_total)
    orders = jax.vmap(lambda one_key: jax.random.permutation(one_key, REQS))(perm_keys)
    request_index = jnp.arange(REQS)[:, None]
    entry_index = jnp.arange(MAXBLK)[None, :]
    owners = orders[request_index // 4, entry_index % REQS]
    shared = jax.random.randint(key_shared, (group_total, MAXBLK), 0, POOL_DEV)
    own_slots = jax.random.randint(key_own, (REQS, MAXBLK), 0, POOL_DEV)
    slots = jnp.where(entry_index < MAXBLK // 2, shared[request_index // 4, entry_index], own_slots)
    return (owners.astype(jnp.int32), slots.astype(jnp.int32))


def draw_block_owner(key, part):
    return block_tables(key)[0]


def draw_block_slot(key, part):
    return block_tables(key)[1]


def draw_block_count(key, part):
    key = jax.random.fold_in(key, 21)
    key_vals, key_pick = jax.random.split(key)
    counts = jax.random.randint(key_vals, (REQS,), MAXBLK // 2, MAXBLK + 1)
    chosen = jax.random.randint(key_pick, (), 0, REQS)
    return jnp.where(jnp.arange(REQS) == chosen, MAXBLK, counts).astype(jnp.int32)


def draw_suffix_len(key, part):
    key = jax.random.fold_in(key, 23)
    key_vals, key_pick = jax.random.split(key)
    lengths = jax.random.randint(key_vals, (REQS,), SUFFIX // 4, SUFFIX + 1)
    chosen = jax.random.randint(key_pick, (), 0, REQS)
    return jnp.where(jnp.arange(REQS) == chosen, SUFFIX, lengths).astype(jnp.int32)


def draw_decay_log(key, part):
    key = jax.random.fold_in(key, 13)
    key_perm, key_unif = jax.random.split(key)
    ranks = jax.random.permutation(key_perm, MHEADS)
    slow_total = MHEADS // 2
    unit = jax.random.uniform(key_unif, (MHEADS,), jnp.float32, 0.0, 1.0)
    slow_rate = 0.5 / SUFFIX * jnp.exp(unit * 1.8)
    fast_rate = 0.05 * jnp.exp(unit * 1.1)
    rates = jnp.where(ranks < slow_total, slow_rate, fast_rate)
    return jnp.log(rates).astype(jnp.float32)


def draw_queries(key, part):
    key = jax.random.fold_in(key, 11)
    shape = (REQS, SUFFIX, QHEADS * ATT_DIM)
    values = jnp.clip(jax.random.normal(key, shape, jnp.float32), -5.0, 5.0)
    return values.astype(jnp.bfloat16)


def draw_block_pool(key, part):
    key = jax.random.fold_in(key, 17)
    shape = (POOL, BLOCK, KVHEADS, 2 * ATT_DIM)
    values = jnp.clip(jax.random.normal(key, shape, jnp.float32), -5.0, 5.0)
    return values.astype(jnp.bfloat16)


def set_ends(result, own_key, low, top_value):
    dims = result.shape
    place = [jax.random.randint(jax.random.fold_in(own_key, axis), (), 0, dims[axis]) for axis in range(len(dims))]
    result = result.at[tuple(place)].set(low)
    longest = dims.index(max(dims))
    place[longest] = (place[longest] + 1) % dims[longest]
    return result.at[tuple(place)].set(top_value)


def block_scale(key, dims, shards, least, high):
    factor_of = 1.0
    for dim, parts in shards:
        steps = jax.random.uniform(jax.random.fold_in(jax.random.fold_in(key, 6), dim), (parts,), jnp.float32, least / len(shards), high / len(shards))
        factor_of = factor_of * jnp.repeat(jnp.exp(steps), dims[dim] // parts).reshape((-1,) + (1,) * (len(dims) - 1 - dim))
    return factor_of


def scatter_about(stream_key, dims, deviation, reach, cuts=(), kind=jnp.bfloat16):
    values = jax.random.normal(stream_key, dims, jnp.float32) * deviation
    if len(cuts) > 0:
        values = block_scale(stream_key, dims, cuts, -0.22, 0.18) * values
    return jnp.clip(values, min=-reach, max=reach).astype(kind)


def setup_inputs(seed: int = 0) -> dict:
    splits = jax.random.split(jax.random.key(seed), 18)
    return {
        "ssm_input": scatter_about(splits[0], (REQS, SUFFIX, MHEADS * HEAD_DIM), 1.0, 6.0, ((0, 32), (1, 8))),
        "ssm_gate": scatter_about(splits[1], (REQS, SUFFIX, MHEADS * HEAD_DIM), 1.0, 6.0, ((0, 32), (1, 8))),
        "state_proj": scatter_about(splits[2], (REQS, SUFFIX, 2 * GROUPS * STATE), 0.3, 1.796875, ((0, 32), (1, 8))),
        "step_raw": scatter_about(splits[3], (REQS, SUFFIX, MHEADS), 0.5, 3.0, ((0, 32), (1, 8))),
        "queries": draw_queries(jax.random.fold_in(splits[17], 71), 0),
        "fresh_kv": scatter_about(splits[5], (REQS, SUFFIX, 2 * KVHEADS * ATT_DIM), 1.0, 6.0, ((0, 32), (1, 8))),
        "block_pool": draw_block_pool(jax.random.fold_in(splits[17], 71), 0),
        "state_pool": scatter_about(splits[7], (ENTRIES, MHEADS, HEAD_DIM, STATE), 4.0, 16.0, ((0, 32), (1, 8))),
        "decay_log": draw_decay_log(jax.random.fold_in(splits[17], 71), 0),
        "step_bias": jnp.clip(-1.0 + 1.0 * jax.random.uniform(splits[9], (MHEADS,), jnp.float32) ** block_scale(splits[9], (MHEADS,), ((0, 8),), -0.2, 0.2), -1.0, 0.0),
        "skip_gain": jnp.clip(1.0 + 2.0 * jax.random.uniform(splits[10], (MHEADS,), jnp.float32) ** block_scale(splits[10], (MHEADS,), ((0, 8),), -0.2, 0.2), 1.0, 3.0),
        "norm_gain": jnp.clip(1.0 + 0.1 * jax.random.normal(splits[11], (MHEADS * HEAD_DIM,), jnp.float32), 0.5, 1.5),
        "block_owner": draw_block_owner(jax.random.fold_in(splits[17], 71), 0),
        "block_slot": draw_block_slot(jax.random.fold_in(splits[17], 71), 0),
        "block_count": draw_block_count(jax.random.fold_in(splits[17], 71), 0),
        "state_entry": set_ends(jax.random.randint(splits[15], (REQS,), 0, ENTRIES), jax.random.fold_in(splits[15], 1), 0, ENTRIES - 1).astype(jnp.int32),
        "suffix_len": draw_suffix_len(jax.random.fold_in(splits[17], 71), 0),
    }


HIGH = lax.Precision.HIGHEST

def rounded(value):
    return lax.optimization_barrier(value.astype(jnp.bfloat16)).astype(jnp.float32)

def scan_heads(ssm_rows, gate_rows, proj_rows, step_rows, initial, decay_log, step_bias, skip_gain, norm_gain, live_len, group_count):
    length_all, width = ssm_rows.shape
    head_count = step_rows.shape[1]
    head_size = width // head_count
    per_group = head_count // group_count
    state_size = proj_rows.shape[1] // (2 * group_count)
    block_count = length_all // SPAN
    inputs = ssm_rows.astype(jnp.float32).reshape(block_count, SPAN, group_count, per_group, head_size)
    proj_four = proj_rows.astype(jnp.float32).reshape(block_count, SPAN, group_count, 2, state_size)
    in_proj = proj_four[:, :, :, 0]
    out_proj = proj_four[:, :, :, 1]
    step_size = jax.nn.softplus(step_rows.astype(jnp.float32) + step_bias[None, :])
    step_size = step_size.reshape(block_count, SPAN, group_count, per_group)
    rates = jnp.exp(decay_log).reshape(group_count, per_group)
    skip_heads = skip_gain.reshape(group_count, per_group)
    lower = jnp.arange(SPAN)[:, None] >= jnp.arange(SPAN)[None, :]

    def advance(state, block_in):
        block_x, block_b, block_c, block_dt = block_in
        cumul = jnp.cumsum(-rates[None] * block_dt, axis=0)
        inner = jnp.einsum('tgn,ugn->tug', block_c, block_b, precision=HIGH)
        spread = cumul[:, None] - cumul[None, :]
        decay = jnp.exp(jnp.where(lower[:, :, None, None], spread, -jnp.inf))
        mixing = rounded(decay * inner[:, :, :, None] * block_dt[None])
        output = jnp.einsum('tugh,ughp->tghp', mixing, block_x, precision=HIGH)
        state_in = rounded(state)
        carried = jnp.einsum('tgn,ghpn->tghp', block_c, state_in, precision=HIGH)
        output = output + jnp.exp(cumul)[..., None] * carried
        output = output + skip_heads[None, :, :, None] * block_x
        tail_weight = jnp.exp(cumul[-1][None] - cumul) * block_dt
        tail_terms = rounded(tail_weight[..., None] * block_x)
        state = jnp.exp(cumul[-1])[:, :, None, None] * state + jnp.einsum('ughp,ugn->ghpn', tail_terms, block_b, precision=HIGH)
        return (state, output)
    start_state = initial.reshape(group_count, per_group, head_size, state_size)
    final_state, outputs = lax.scan(advance, start_state, (inputs, in_proj, out_proj, step_size))
    outputs = outputs.reshape(length_all, group_count, per_group * head_size)
    gated = outputs * jax.nn.silu(gate_rows.astype(jnp.float32)).reshape(length_all, group_count, per_group * head_size)
    mean_sq = lax.optimization_barrier(jnp.mean(gated * gated, axis=-1, keepdims=True))
    normed = gated * lax.rsqrt(mean_sq + 1e-05) * norm_gain.reshape(group_count, per_group * head_size)
    normed = normed.reshape(length_all, width)
    alive = jnp.arange(length_all) < live_len
    return jnp.where(alive[:, None], normed, 0.0).astype(jnp.bfloat16)

def attend(query_rows, key_rows, value_rows, prefix_live, live_len):
    length_all, kv_count, repeat, head_size = query_rows.shape
    key_total = key_rows.shape[0]
    prefix_rows = key_total - length_all
    rows_block = min(256, length_all)
    inv_root = 1.0 / head_size ** 0.5
    key_index = jnp.arange(key_total)
    keys_wide = key_rows.astype(jnp.float32)
    values_wide = value_rows.astype(jnp.float32)

    def one_block(offset):
        block_q = lax.dynamic_slice_in_dim(query_rows, offset, rows_block, 0).astype(jnp.float32)
        scores = jnp.einsum('qcrd,kcd->crqk', block_q, keys_wide) * inv_root
        query_index = offset + jnp.arange(rows_block)
        allowed = jnp.where(key_index[None, :] < prefix_rows, key_index[None, :] < prefix_live, key_index[None, :] - prefix_rows <= query_index[:, None])
        scores = jnp.where(allowed[None, None], scores, -jnp.inf)
        row_max = lax.optimization_barrier(jnp.max(scores, axis=-1, keepdims=True))
        expon = jnp.exp(scores - row_max)
        totals = lax.optimization_barrier(jnp.sum(expon, axis=-1))
        weights = expon.astype(jnp.bfloat16).astype(jnp.float32)
        mixed = jnp.einsum('crqk,kcd->qcrd', weights, values_wide)
        mixed = mixed / jnp.transpose(totals, (2, 0, 1))[..., None]
        mixed = jnp.where((query_index < live_len)[:, None, None, None], mixed, 0.0)
        return mixed.astype(jnp.bfloat16)
    outputs = lax.map(one_block, jnp.arange(length_all // rows_block, dtype=jnp.int32) * rows_block)
    return outputs.reshape(length_all, kv_count * repeat * head_size)

def reference(ssm_input, ssm_gate, state_proj, step_raw, queries, fresh_kv, block_pool, state_pool, decay_log, step_bias, skip_gain, norm_gain, block_owner, block_slot, block_count, state_entry, suffix_len):

    def one_request(request):
        initial = state_pool[state_entry[request]].astype(jnp.float32)
        mamba = scan_heads(ssm_input[request], ssm_gate[request], state_proj[request], step_raw[request], initial, decay_log, step_bias, skip_gain, norm_gain, suffix_len[request], GROUPS)
        block_ids = (block_owner[request] * POOL_DEV + block_slot[request]).astype(jnp.int32)
        cached = block_pool[block_ids].reshape(MAXBLK * BLOCK, KVHEADS, 2 * ATT_DIM)
        newest = fresh_kv[request].reshape(SUFFIX, KVHEADS, 2 * ATT_DIM)
        joined = jnp.concatenate([cached, newest], axis=0)
        query_rows = queries[request].reshape(SUFFIX, KVHEADS, QHEADS // KVHEADS, ATT_DIM)
        attention = attend(query_rows, joined[..., :ATT_DIM], joined[..., ATT_DIM:], block_count[request] * BLOCK, suffix_len[request])
        return (mamba, attention)
    ssm_out, attn_out = lax.map(one_request, jnp.arange(REQS, dtype=jnp.int32))
    return (ssm_out, attn_out)
```

```python
import jax
import jax.numpy as jnp
from jax import lax
from jax.experimental import pallas as pl
from jax.experimental.pallas import tpu as pltpu
from jax.sharding import PartitionSpec as P

MESH = pl.DeviceIdType.MESH
F32 = jnp.float32
BF16 = jnp.bfloat16

NZ, NY, NT = 8, 4, 8
ROWS = 64
SPAN = 256
CHUNKS = 4
DIST = (0, 1, 2, 3, 4, -1, -2, -3)
LOW = -1e30
SCALE = 1.4426950408889634 / 128**0.5


def dot(a, b, dims=(((1,), (0,)), ((), ())), precision=None):
    return lax.dot_general(a, b, dims, precision=precision, preferred_element_type=F32)


BT = (((1,), (1,)), ((), ()))
AT = (((0,), (0,)), ((), ()))


def kernel(
    tab,
    bias,
    par,
    gain,
    step,
    proj,
    xin,
    query,
    fresh,
    gate,
    pool,
    state,
    ssm_out,
    attn_out,
    stepb,
    gainb,
    projb,
    xb,
    qb,
    fb,
    gateb,
    kz,
    ksend,
    kvb,
    yb,
    tk,
    ts,
    cum_c,
    dt_c,
    w_c,
    cum_r,
    dt_r,
    inner,
    yint,
    ecx,
    tailb,
    osend,
    ob,
    m_s,
    l_s,
    acc_s,
    ao,
    lsem,
    xs,
    xr,
    kzs,
    kzr,
    kys,
    kyr,
    sys_,
    syr,
    tss,
    tsr,
    oss,
    osr,
    aos,
    aor,
):
    r = lax.axis_index("req")
    p = lax.axis_index("tp")
    z = r // NY
    y = lax.rem(r, NY)

    def tp_of(d):
        return lax.rem(p + d, NT)

    def z_of(k):
        return lax.rem(z + k + 2 * NZ, NZ)

    def y_of(k):
        return lax.rem(y + k + NY, NY)

    def remote(src, dst, ssem, rsem, device):
        return pltpu.make_async_remote_copy(
            src_ref=src, dst_ref=dst, send_sem=ssem, recv_sem=rsem, device_id=device, device_id_type=MESH
        )

    barrier = pltpu.get_barrier_semaphore()
    peers = [(r, tp_of(d)) for d in range(1, NT)]
    peers += [(z_of(1) * NY + y, p), (z_of(-1) * NY + y, p)]
    peers += [(z * NY + y_of(j), p) for j in range(1, NY)]
    for peer in peers:
        pl.semaphore_signal(barrier, inc=1, device_id=peer, device_id_type=MESH)
    pl.semaphore_wait(barrier, len(peers))

    pending = []
    local = []

    def start(copy):
        copy.start()
        pending.append(copy)
        return copy

    def start_local(src, dst):
        copy = pltpu.make_async_copy(src, dst, lsem.at[len(local)])
        copy.start()
        local.append(copy)
        return copy

    my_rows = pl.ds(pl.multiple_of(p * ROWS, ROWS), ROWS)

    def spread(i, src, dst, width):
        out = [start_local(src.at[:, pl.ds(pl.multiple_of(p * width, 128), width)], dst.at[my_rows, :])]
        for d in range(1, NT):
            to = tp_of(d)
            out.append(
                start(
                    remote(
                        src.at[:, pl.ds(pl.multiple_of(to * width, 128), width)],
                        dst.at[my_rows, :],
                        xs.at[i, d - 1],
                        xr.at[i, d - 1],
                        (r, to),
                    )
                )
            )
        return out

    def everyone(i, src, dst):
        out = [start_local(src, dst)]
        for d in range(1, NT):
            out.append(start(remote(src, dst, xs.at[i, d - 1], xr.at[i, d - 1], (r, tp_of(d)))))
        return out

    def arrive(copies):
        copies[0].wait()
        for copy in copies[1:]:
            copy.wait_recv()

    def gather_state(c):
        out = [start_local(state.at[c], yb[c].at[y])]
        for j in range(1, NY):
            out.append(
                start(
                    remote(
                        state.at[c],
                        yb[c].at[y],
                        sys_.at[c, j - 1],
                        syr.at[c, j - 1],
                        (z * NY + y_of(j), p),
                    )
                )
            )
        return out

    def kv_hop(s, way):
        slot = s if way > 0 else 4 + s
        before = pool if s == 1 else kz[slot - 1]
        return start(
            remote(before, kz[slot], kzs.at[slot], kzr.at[slot], (z_of(way) * NY + y, p))
        )

    kv_copies = {}

    def kv_across(k):
        for j in range(NY):
            to = y_of(j)
            first = kz[k][tab[0, to * 32 + k * 4 + y]]
            second = kz[k][tab[1, to * 32 + k * 4 + y]]
            if j == 0:
                kvb[y, k, 0] = first
                kvb[y, k, 1] = second
            else:
                ksend[k, j - 1, 0] = first
                ksend[k, j - 1, 1] = second
                kv_copies[k, j] = start(
                    remote(
                        ksend.at[k, j - 1],
                        kvb.at[y, k],
                        kys.at[k, j - 1],
                        kyr.at[k, j - 1],
                        (z * NY + to, p),
                    )
                )

    kv_hops = {}

    def kv_step(s):
        kv_hops[s, 1].wait_recv()
        if s < 4:
            kv_hops[s + 1, 1] = kv_hop(s + 1, 1)
        if s <= 3:
            kv_hops[s, -1].wait_recv()
            if s < 3:
                kv_hops[s + 1, -1] = kv_hop(s + 1, -1)
        kv_across(s)
        if s <= 3:
            kv_across(4 + s)

    gathers = {}
    tokens = {}

    def length(c, way):
        return 4 if (way > 0) == (c % 2 == 0) else 3

    def tok_hop(c, s, way):
        total = length(c, way)
        dest = z_of(way * (total - s + 1))
        base = 0 if way > 0 else 4
        mine = yb[c][tab[2, 8 + dest]]
        if s > 1:
            mine = jnp.where(tab[2, dest] == z, mine, tk[c][base + s - 2])
        ts[c][base + s - 1] = mine
        tokens[c, s, way] = start(
            remote(
                ts[c].at[base + s - 1],
                tk[c].at[base + s - 1],
                tss.at[c, base + s - 1],
                tsr.at[c, base + s - 1],
                (z_of(way) * NY + y, p),
            )
        )

    def tok_step(c, s):
        if s == 0:
            arrive(gathers[c])
            tok_hop(c, 1, 1)
            tok_hop(c, 1, -1)
            return
        for way in (1, -1):
            if s <= length(c, way):
                tokens[c, s, way].wait_recv()
                if s < length(c, way):
                    tok_hop(c, s + 1, way)

    gathers[0] = gather_state(0)
    kv_hops[1, 1] = kv_hop(1, 1)
    kv_hops[1, -1] = kv_hop(1, -1)
    in_step = everyone(0, step, stepb.at[my_rows, :])
    in_proj = spread(1, proj, projb, 512)
    in_x = spread(2, xin, xb, 1024)
    own_pool = start_local(pool, kz[0])
    in_gate = start_local(gate, gateb)
    own_pool.wait()
    kv_across(0)
    gathers[1] = gather_state(1)
    in_q = spread(3, query, qb, 512)
    in_f = spread(4, fresh, fb, 256)
    in_gain = everyone(5, gain, gainb.at[p])
    live = tab[2, 16]

    kv_step(1)
    kv_step(2)
    tok_step(0, 0)
    gathers[2] = gather_state(2)
    kv_step(3)
    tok_step(0, 1)

    arrive(in_step)
    take = (
        lax.broadcasted_iota(jnp.int32, (128, 128), 0)
        == lax.broadcasted_iota(jnp.int32, (128, 128), 1) + p * 16
    ).astype(BF16)
    raw = dot(stepb[...], take) + par[1:2, 0:128]
    dt = jnp.maximum(raw, 0.0) + jnp.log1p(jnp.exp(-jnp.abs(raw)))
    drop = dt * -jnp.exp(par[2:3, 0:128])
    lower = lax.broadcasted_iota(jnp.int32, (SPAN, SPAN), 0) >= lax.broadcasted_iota(
        jnp.int32, (SPAN, SPAN), 1
    )
    ones = lower.astype(F32)
    dt_c[...] = dt
    for b in range(2):
        rows = slice(b * SPAN, (b + 1) * SPAN)
        cum = dot(ones, drop[rows], precision=lax.Precision.HIGHEST)
        cum_c[rows, :] = cum
        cum_r[b] = cum.T
        dt_r[b] = dt[rows].T
        if b == 0:
            w_c[...] = jnp.exp(cum[SPAN - 1 : SPAN] - cum) * dt[rows]
    arrive(in_proj)
    for b in range(2):
        rows = slice(b * SPAN, (b + 1) * SPAN)
        inner[b] = dot(projb[rows, 256:512], projb[rows, 0:256], BT)
    arrive(in_x)

    half = lax.broadcasted_iota(jnp.int32, (SPAN, 128), 1) < 64

    def pair(hp, carry):
        cols = pl.ds(pl.multiple_of(hp * 128, 128), 128)
        for b in range(2):
            rows = slice(b * SPAN, (b + 1) * SPAN)
            xp = xb[rows, cols]
            cum_b = cum_c[rows, :]
            res, cumcols, weights = [], [], []
            for e in range(2):
                h = hp * 2 + e
                column = pltpu.roll(cum_b, 128 - h, 1)[:, 0:1]
                spread_cum = column - cum_r[b, pl.ds(h, 1), :]
                mix = jnp.exp(jnp.where(lower, spread_cum, LOW)) * inner[b] * dt_r[b, pl.ds(h, 1), :]
                res.append(dot(mix.astype(BF16), xp))
                cumcols.append(column)
                if b == 0:
                    weights.append(pltpu.roll(w_c[...], 128 - h, 1)[:, 0:1])
            xf = xp.astype(F32)
            ecx[rows, cols] = jnp.exp(jnp.where(half, cumcols[0], cumcols[1]))
            yint[rows, cols] = jnp.where(half, res[0], res[1]) + par[0:1, cols] * xf
            if b == 0:
                tailb[:, cols] = (jnp.where(half, weights[0], weights[1]) * xf).astype(BF16)
        return carry

    kv_step(4)
    tok_step(0, 2)
    tok_step(1, 0)
    gathers[3] = gather_state(3)
    lax.fori_loop(0, 4, pair, 0)
    tok_step(0, 3)
    tok_step(1, 1)
    lax.fori_loop(4, 8, pair, 0)

    def wait_out(copies):
        for copy in copies:
            copy.wait_recv()

    ssm_sends = {}

    def carry_in(c):
        ze = tab[2, z]
        behind = lax.rem(z - ze + NZ, NZ)
        entering = jnp.where(
            behind <= length(c, 1), tk[c][length(c, 1) - 1], tk[c][4 + length(c, -1) - 1]
        )
        s0 = jnp.where(ze == z, yb[c][tab[2, 8 + z]], entering)
        cols = slice(c * 256, (c + 1) * 256)
        eye = (
            lax.broadcasted_iota(jnp.int32, (256, 256), 0) == lax.broadcasted_iota(jnp.int32, (256, 256), 1)
        ).astype(BF16)
        s0t = dot(eye, s0, BT)
        s1t = ecx[SPAN - 1 : SPAN, cols] * s0t + dot(projb[0:SPAN, 0:256], tailb[:, cols], AT)
        for b, st in ((0, s0t), (1, s1t)):
            rows = slice(b * SPAN, (b + 1) * SPAN)
            carried = dot(projb[rows, 256:512], st.astype(BF16))
            osend[c, rows, :] = (yint[rows, cols] + ecx[rows, cols] * carried).astype(BF16)
        out = []
        for d in range(1, NT):
            to = tp_of(d)
            out.append(
                start(
                    remote(
                        osend.at[c, pl.ds(pl.multiple_of(to * ROWS, ROWS), ROWS), :],
                        ob.at[c, my_rows, :],
                        oss.at[c, d - 1],
                        osr.at[c, d - 1],
                        (r, to),
                    )
                )
            )
        ob[c, my_rows, :] = osend[c, my_rows, :]
        ssm_sends[c] = out

    tok_step(0, 4)
    tok_step(1, 2)
    tok_step(2, 0)
    carry_in(0)

    arrive(in_q)
    arrive(in_f)

    def attend_fresh(i, carry):
        head = i // 2
        tile = lax.rem(i, 2)
        qt = qb[pl.ds(pl.multiple_of(tile * 256, 256), 256), pl.ds(pl.multiple_of(head * 128, 128), 128)]
        s = dot(qt, fb[:, 0:128], BT)
        allowed = lax.broadcasted_iota(jnp.int32, (256, 512), 1) <= (
            lax.broadcasted_iota(jnp.int32, (256, 512), 0) + tile * 256
        )
        s = jnp.where(allowed, s, LOW)
        top = jnp.max(s, axis=1, keepdims=True)
        w = jnp.exp2((s - top) * SCALE)
        m_s[i] = jnp.broadcast_to(top, (256, 128))
        l_s[i] = jnp.broadcast_to(jnp.sum(w, axis=1, keepdims=True), (256, 128))
        acc_s[i] = dot(w.astype(BF16), fb[:, 128:256])
        return carry

    lax.fori_loop(0, 8, attend_fresh, 0)

    def attend_cached(j):
        owner = y_of(-j)
        if j > 0:
            for k in range(8):
                kv_copies[k, j].wait_recv()

        def tile_of(i, carry):
            head = i // 2
            tile = lax.rem(i, 2)
            qt = qb[
                pl.ds(pl.multiple_of(tile * 256, 256), 256), pl.ds(pl.multiple_of(head * 128, 128), 128)
            ]
            block = kvb[owner].reshape(1024, 256)
            s = dot(qt, block[:, 0:128], BT) + bias[owner]
            old = m_s[i][:, 0:1]
            top = jnp.maximum(old, jnp.max(s, axis=1, keepdims=True))
            w = jnp.exp2((s - top) * SCALE)
            fade = jnp.exp2((old - top) * SCALE)
            m_s[i] = jnp.broadcast_to(top, (256, 128))
            l_s[i] = l_s[i] * fade + jnp.sum(w, axis=1, keepdims=True)
            acc_s[i] = acc_s[i] * fade + dot(w.astype(BF16), block[:, 128:256])
            return carry

        lax.fori_loop(0, 8, tile_of, 0)

    attend_cached(0)
    tok_step(1, 3)
    tok_step(2, 1)
    attend_cached(1)
    tok_step(1, 4)
    tok_step(2, 2)
    tok_step(3, 0)
    carry_in(1)
    attend_cached(2)
    tok_step(2, 3)
    tok_step(3, 1)
    attend_cached(3)

    def finish(i, carry):
        head = i // 2
        tile = lax.rem(i, 2)
        alive = lax.broadcasted_iota(jnp.int32, (256, 128), 0) + tile * 256 < live
        value = jnp.where(alive, acc_s[i] / l_s[i], 0.0)
        ao[
            pl.ds(pl.multiple_of(tile * 256, 256), 256), pl.ds(pl.multiple_of(head * 128, 128), 128)
        ] = value.astype(BF16)
        return carry

    lax.fori_loop(0, 8, finish, 0)
    my_cols = pl.ds(pl.multiple_of(p * 512, 512), 512)
    attn_sends = []
    for d in range(1, NT):
        to = tp_of(d)
        attn_sends.append(
            start(
                remote(
                    ao.at[pl.ds(pl.multiple_of(to * ROWS, ROWS), ROWS), :],
                    attn_out.at[:, my_cols],
                    aos.at[d - 1],
                    aor.at[d - 1],
                    (r, to),
                )
            )
        )
    own_attn = start_local(ao.at[my_rows, :], attn_out.at[:, my_cols])

    tok_step(2, 4)
    tok_step(3, 2)
    carry_in(2)
    tok_step(3, 3)
    tok_step(3, 4)
    carry_in(3)

    in_gate.wait()
    arrive(in_gain)
    for c in range(CHUNKS):
        wait_out(ssm_sends[c])

    def norm(g, carry):
        rows = pl.ds(pl.multiple_of(g * ROWS, ROWS), ROWS)
        parts = []
        square = jnp.zeros((ROWS, 1), F32)
        for c in range(CHUNKS):
            cols = pl.ds(pl.multiple_of(g * 1024 + c * 256, 256), 256)
            gv = gateb[:, cols].astype(F32)
            gated = ob[c, rows, :].astype(F32) * (gv / (1.0 + jnp.exp(-gv)))
            parts.append(gated)
            square = square + jnp.sum(gated * gated, axis=1, keepdims=True)
        factor = lax.rsqrt(square * (1.0 / 1024) + 1e-5)
        alive = lax.broadcasted_iota(jnp.int32, (ROWS, 1), 0) + p * ROWS < live
        factor = jnp.where(alive, factor, 0.0)
        gains = gainb[g]
        for c in range(CHUNKS):
            for e in range(2):
                k = c * 2 + e
                ssm_out[:, pl.ds(pl.multiple_of(g * 1024 + k * 128, 128), 128)] = (
                    parts[c][:, e * 128 : (e + 1) * 128] * factor * gains[k : k + 1, :]
                ).astype(BF16)
        return carry

    lax.fori_loop(0, NT, norm, 0)

    own_attn.wait()
    for copy in attn_sends:
        copy.wait_recv()
    for copy in pending:
        copy.wait_send()


def run(tab, bias, par, gain, step, proj, xin, query, fresh, gate, pool, state):
    any_ = pl.BlockSpec(memory_space=pl.ANY)
    vmem = pl.BlockSpec(memory_space=pltpu.VMEM)
    smem = pl.BlockSpec(memory_space=pltpu.SMEM)
    dma = pltpu.SemaphoreType.DMA
    return pl.pallas_call(
        kernel,
        out_shape=(
            jax.ShapeDtypeStruct((ROWS, 8192), BF16),
            jax.ShapeDtypeStruct((ROWS, 4096), BF16),
        ),
        in_specs=[smem, vmem, vmem] + [any_] * 9,
        out_specs=(vmem, any_),
        scratch_shapes=[
            pltpu.VMEM((512, 128), BF16),
            pltpu.VMEM((NT, 8, 128), F32),
            pltpu.VMEM((512, 512), BF16),
            pltpu.VMEM((512, 1024), BF16),
            pltpu.VMEM((512, 512), BF16),
            pltpu.VMEM((512, 256), BF16),
            pltpu.VMEM((ROWS, 8192), BF16),
            [pltpu.VMEM((4, 64, 256), BF16)] * 8,
            pltpu.VMEM((8, 3, 2, 64, 256), BF16),
            pltpu.VMEM((NY, 8, 2, 64, 256), BF16),
            [pltpu.VMEM((NY, 256, 256), BF16)] * CHUNKS,
            [pltpu.VMEM((8, 256, 256), BF16)] * CHUNKS,
            [pltpu.VMEM((8, 256, 256), BF16)] * CHUNKS,
            pltpu.VMEM((512, 128), F32),
            pltpu.VMEM((512, 128), F32),
            pltpu.VMEM((256, 128), F32),
            pltpu.VMEM((2, 128, 256), F32),
            pltpu.VMEM((2, 128, 256), F32),
            pltpu.VMEM((2, 256, 256), F32),
            pltpu.VMEM((512, 1024), F32),
            pltpu.VMEM((512, 1024), F32),
            pltpu.VMEM((256, 1024), BF16),
            pltpu.VMEM((CHUNKS, 512, 256), BF16),
            pltpu.VMEM((CHUNKS, 512, 256), BF16),
            pltpu.VMEM((8, 256, 128), F32),
            pltpu.VMEM((8, 256, 128), F32),
            pltpu.VMEM((8, 256, 128), F32),
            pltpu.VMEM((512, 512), BF16),
            dma((16,)),
            dma((6, 7)),
            dma((6, 7)),
            dma((8,)),
            dma((8,)),
            dma((8, 3)),
            dma((8, 3)),
            dma((CHUNKS, 3)),
            dma((CHUNKS, 3)),
            dma((CHUNKS, 8)),
            dma((CHUNKS, 8)),
            dma((CHUNKS, 7)),
            dma((CHUNKS, 7)),
            dma((7,)),
            dma((7,)),
        ],
        compiler_params=pltpu.CompilerParams(
            collective_id=0, has_side_effects=True, vmem_limit_bytes=56 * 2**20
        ),
        name="prefill",
    )(tab, bias, par, gain, step, proj, xin, query, fresh, gate, pool, state)


def per_device(
    ssm_input,
    ssm_gate,
    state_proj,
    step_raw,
    queries,
    fresh_kv,
    block_pool,
    state_pool,
    decay_log,
    step_bias,
    skip_gain,
    norm_gain,
    block_owner,
    block_slot,
    block_count,
    state_entry,
    suffix_len,
):
    r = lax.axis_index("req")
    z = r // NY
    y = r % NY
    owner4 = lax.dynamic_slice(block_owner, (z * NY, 0), (NY, 64))
    slot4 = lax.dynamic_slice(block_slot, (z * NY, 0), (NY, 64))
    count4 = lax.dynamic_slice(block_count, (z * NY,), (NY,))
    place = jnp.arange(64, dtype=jnp.int32)
    code = place[None, :] * 4 + slot4
    dist = jnp.array(DIST, jnp.int32)
    owners = ((z - dist + NZ) % NZ)[:, None] * NY + jnp.arange(NY, dtype=jnp.int32)[None, :]
    named = (owner4[:, None, None, :] == owners[None, :, :, None]) & (
        place[None, :] < count4[:, None]
    )[:, None, None, :]
    first = jnp.min(jnp.where(named, code[:, None, None, :], 1024), axis=-1)
    last = jnp.max(jnp.where(named, code[:, None, None, :], -1), axis=-1)
    slot_first = jnp.where(first < 1024, first & 3, 0)
    slot_last = jnp.where(last >= 0, last & 3, 0)
    live = lax.dynamic_slice(suffix_len, (r,), (1,))
    column = state_entry.reshape(NZ, NY)
    entries = lax.dynamic_slice(column, (0, y), (NZ, 1))[:, 0]
    misc = jnp.concatenate([entries // NY, entries % NY, live, jnp.zeros((111,), jnp.int32)])
    tab = jnp.stack([slot_first.reshape(128), slot_last.reshape(128), misc])
    mine_first = lax.dynamic_index_in_dim(first, y, 0, keepdims=False)
    mine_last = lax.dynamic_index_in_dim(last, y, 0, keepdims=False)
    valid = jnp.stack([mine_first < 1024, mine_last > mine_first], axis=-1)
    bias = jnp.where(valid.transpose(1, 0, 2), 0.0, LOW).astype(F32)
    bias = jnp.repeat(bias.reshape(NY, 1, 16), 64, axis=2)
    par = jnp.stack(
        [
            jnp.repeat(skip_gain, 64),
            jnp.pad(step_bias, (0, 1008)),
            jnp.pad(decay_log, (0, 1008)),
        ]
    )
    ssm, attn = run(
        tab,
        bias,
        par,
        norm_gain.reshape(8, 128),
        step_raw[0],
        state_proj[0],
        ssm_input[0],
        queries[0],
        fresh_kv[0],
        ssm_gate[0],
        block_pool.reshape(4, 64, 256),
        state_pool.reshape(CHUNKS, 256, 256),
    )
    return (ssm[None], attn[None])


def solution(mesh):
    return jax.shard_map(
        per_device,
        mesh=mesh,
        in_specs=(
            P("req", "tp", None),
            P("req", "tp", None),
            P("req", "tp", None),
            P("req", "tp", None),
            P("req", "tp", None),
            P("req", "tp", None),
            P("req", None, "tp", None),
            P("req", "tp", None, None),
            P("tp"),
            P("tp"),
            P("tp"),
            P("tp"),
            P(),
            P(),
            P(),
            P(),
            P(),
        ),
        out_specs=(P("req", "tp", None), P("req", "tp", None)),
        check_vma=False,
    )
```

```python
import jax
import jax.numpy as jnp
from jax import lax
from jax.experimental import pallas as pl
from jax.experimental.pallas import tpu as pltpu
from jax.sharding import PartitionSpec as P

MESH = pl.DeviceIdType.MESH
F32 = jnp.float32
BF16 = jnp.bfloat16

NZ, NY, NT = 8, 4, 8
ROWS = 64
SPAN = 256
PARTS = 8
FLIGHT = 4
DIST = (0, 1, -1, 2, -2, 3, -3, 4)
LOW = -1e30
SCALE = 1.4426950408889634 / 128**0.5


def dot(a, b, dims=(((1,), (0,)), ((), ())), precision=None):
    return lax.dot_general(a, b, dims, precision=precision, preferred_element_type=F32)


BT = (((1,), (1,)), ((), ()))
AT = (((0,), (0,)), ((), ()))


def kernel(
    owner_in,
    slot_in,
    count_in,
    entry_in,
    suffix_in,
    decay_in,
    bias_in,
    skip_in,
    gain,
    step,
    proj,
    xin,
    query,
    fresh,
    gate,
    pool,
    state,
    ssm_out,
    attn_out,
    owner,
    slot,
    count,
    entry,
    suffix,
    decay_log,
    step_bias,
    skip_gain,
    tabv,
    tabs,
    bias,
    stepb,
    gainb,
    projb,
    xb,
    qb,
    fb,
    gateb,
    gact,
    add_s,
    kz,
    ksend,
    kvb,
    yb,
    tk,
    ts,
    cum_c,
    w_c,
    cum_r,
    dt_r,
    inner,
    yint,
    ecx,
    tailb,
    osend,
    ob,
    m_s,
    l_s,
    acc_s,
    ao,
    tsem,
    lsem,
    xs,
    xr,
    kzs,
    kzr,
    kys,
    kyr,
    sys_,
    syr,
    tss,
    tsr,
    oss,
    osr,
    aos,
    aor,
):
    r = lax.axis_index("req")
    p = lax.axis_index("tp")
    z = r // NY
    y = lax.rem(r, NY)

    def tp_of(d):
        return lax.rem(p + d, NT)

    def z_of(k):
        return lax.rem(z + k + 2 * NZ, NZ)

    def y_of(k):
        return lax.rem(y + k + NY, NY)

    def remote(src, dst, ssem, rsem, device):
        return pltpu.make_async_remote_copy(
            src_ref=src, dst_ref=dst, send_sem=ssem, recv_sem=rsem, device_id=device, device_id_type=MESH
        )

    small = [
        pltpu.make_async_copy(src, dst, tsem.at[1 + i])
        for i, (src, dst) in enumerate(
            (
                (owner_in, owner),
                (slot_in, slot),
                (count_in, count),
                (entry_in, entry),
                (suffix_in, suffix),
                (decay_in, decay_log),
                (bias_in, step_bias),
                (skip_in, skip_gain),
            )
        )
    ]
    for copy in small:
        copy.start()

    barrier = pltpu.get_barrier_semaphore()
    peers = [(r, tp_of(d)) for d in range(1, NT)]
    peers += [(z_of(1) * NY + y, p), (z_of(-1) * NY + y, p)]
    peers += [(z * NY + y_of(j), p) for j in range(1, NY)]
    for peer in peers:
        pl.semaphore_signal(barrier, inc=1, device_id=peer, device_id_type=MESH)

    pending = []
    local = []

    def start(copy):
        copy.start()
        pending.append(copy)
        return copy

    def start_local(src, dst):
        copy = pltpu.make_async_copy(src, dst, lsem.at[len(local)])
        copy.start()
        local.append(copy)
        return copy

    my_rows = pl.ds(pl.multiple_of(p * ROWS, ROWS), ROWS)
    own_pool = start_local(pool, kz[0])

    pl.semaphore_wait(barrier, len(peers))

    def spread(i, src, dst, width):
        out = [start_local(src.at[:, pl.ds(pl.multiple_of(p * width, 128), width)], dst.at[my_rows, :])]
        for d in range(1, NT):
            to = tp_of(d)
            out.append(
                start(
                    remote(
                        src.at[:, pl.ds(pl.multiple_of(to * width, 128), width)],
                        dst.at[my_rows, :],
                        xs.at[i, d - 1],
                        xr.at[i, d - 1],
                        (r, to),
                    )
                )
            )
        return out

    def everyone(i, src, dst):
        out = [start_local(src, dst)]
        for d in range(1, NT):
            out.append(start(remote(src, dst, xs.at[i, d - 1], xr.at[i, d - 1], (r, tp_of(d)))))
        return out

    def arrive(copies):
        copies[0].wait()
        for copy in copies[1:]:
            copy.wait_recv()

    gathers = {}

    def gather_state(c):
        out = [start_local(state.at[c], yb[c].at[y])]
        for j in range(1, NY):
            out.append(
                start(
                    remote(
                        state.at[c],
                        yb[c].at[y],
                        sys_.at[c, j - 1],
                        syr.at[c, j - 1],
                        (z * NY + y_of(j), p),
                    )
                )
            )
        gathers[c] = out

    def length(parity, way):
        return 4 if (way > 0) == (parity == 0) else 3

    hops = {}

    def kv_slot(s, way):
        return DIST.index(s * way) if s < 4 else 7

    def kv_hop(f, s, way):
        slot_now = kv_slot(s, way)
        part = pl.ds(2 * f, 2)
        before = pool if s == 1 else kz[kv_slot(s - 1, way)]
        place = slot_now
        hops[f, s, way] = start(
            remote(
                before.at[part],
                kz[place].at[part],
                kzs.at[f, place],
                kzr.at[f, place],
                (z_of(way) * NY + y, p),
            )
        )

    kv_copies = {}

    def kv_across(k):
        source = lax.rem(z - DIST[k] + NZ, NZ) * NY + y
        for j in range(NY):
            to = y_of(j)
            word = tabs[source, to]
            first = kz[k][lax.rem(word, 4)]
            second = kz[k][lax.rem(lax.div(word, 4), 4)]
            if j == 0:
                kvb[k, y, 0] = first
                kvb[k, y, 1] = second
            else:
                ksend[k, j - 1, 0] = first
                ksend[k, j - 1, 1] = second
                kv_copies[k, j] = start(
                    remote(
                        ksend.at[k, j - 1],
                        kvb.at[k, y],
                        kys.at[k, j - 1],
                        kyr.at[k, j - 1],
                        (z * NY + to, p),
                    )
                )

    def kv_step(f, s):
        for way in (1, -1):
            if s <= length(f, way):
                hops[f, s, way].wait_recv()
                if s < length(f, way):
                    kv_hop(f, s + 1, way)
        if f == 1:
            if s < 4:
                kv_across(DIST.index(s))
                kv_across(DIST.index(-s))
            else:
                kv_across(7)

    tokens = {}

    def tok_hop(c, s, way):
        total = length(c % 2, way)
        dest = z_of(way * (total - s + 1))
        base = 0 if way > 0 else 4
        e = entry[dest * NY + y]
        mine = yb[c][lax.rem(e, NY)]
        if s > 1:
            mine = jnp.where(lax.div(e, NY) == z, mine, tk[c][base + s - 2])
        ts[c][base + s - 1] = mine
        tokens[c, s, way] = start(
            remote(
                ts[c].at[base + s - 1],
                tk[c].at[base + s - 1],
                tss.at[c, base + s - 1],
                tsr.at[c, base + s - 1],
                (z_of(way) * NY + y, p),
            )
        )

    def tok_start(c):
        arrive(gathers[c])
        tok_hop(c, 1, 1)
        tok_hop(c, 1, -1)

    def tok_step(c, s):
        for way in (1, -1):
            if s <= length(c % 2, way):
                tokens[c, s, way].wait_recv()
                if s < length(c % 2, way):
                    tok_hop(c, s + 1, way)

    for f in range(2):
        kv_hop(f, 1, 1)
        kv_hop(f, 1, -1)
    gather_state(0)
    gather_state(1)
    in_step = everyone(0, step, stepb.at[my_rows, :])
    in_proj = spread(1, proj, projb, 512)
    in_x = spread(2, xin, xb, 1024)
    for c in range(2, PARTS):
        gather_state(c)
    in_q = spread(3, query, qb, 512)
    in_f = spread(4, fresh, fb, 256)
    in_gain = everyone(5, gain, gainb.at[p])
    in_gate = start_local(gate, gateb)

    for copy in small:
        copy.wait()
    lane = lax.broadcasted_iota(jnp.int32, (NZ * NY, 64), 1)
    who = lax.broadcasted_iota(jnp.int32, (NZ * NY, 64), 0)
    wide = lax.broadcasted_iota(jnp.int32, (NZ * NY, 128), 1)
    packed = jnp.zeros((NZ * NY, 128), jnp.int32)
    for t in range(NY):
        row = pl.ds(z * NY + t, 1)
        named = (owner[row, :] == who) & (lane < count[z * NY + t])
        code = lane * 4 + slot[row, :]
        first = jnp.min(jnp.where(named, code, 1024), axis=1, keepdims=True)
        last = jnp.max(jnp.where(named, code, -1), axis=1, keepdims=True)
        value = (
            (first & 3)
            + 4 * (last & 3)
            + jnp.where(first < 1024, 16, 0)
            + jnp.where(last > first, 32, 0)
        )
        packed = jnp.where(wide == t, value, packed)
    tabv[...] = packed
    to_scalars = pltpu.make_async_copy(tabv, tabs, tsem.at[0])
    to_scalars.start()

    to_scalars.wait()
    own_pool.wait()
    kv_across(0)
    live = suffix[r]

    side = lax.broadcasted_iota(jnp.int32, (1, 128), 1)
    for k in range(8):
        for t in range(NY):
            word = tabs[lax.rem(z - DIST[k] + NZ, NZ) * NY + t, y]
            flag = jnp.where(side < 64, lax.rem(lax.div(word, 16), 2), lax.div(word, 32))
            place = (k % 2) * 512 + t * 128
            bias[k // 2, :, place : place + 128] = jnp.where(flag > 0, 0.0, LOW)

    lower = lax.broadcasted_iota(jnp.int32, (SPAN, SPAN), 0) >= lax.broadcasted_iota(
        jnp.int32, (SPAN, SPAN), 1
    )
    half = lax.broadcasted_iota(jnp.int32, (SPAN, 128), 1) < 64

    def scan_sums():
        arrive(in_step)
        take = (
            lax.broadcasted_iota(jnp.int32, (128, 128), 0)
            == lax.broadcasted_iota(jnp.int32, (128, 128), 1) + p * 16
        ).astype(BF16)
        shift = jnp.zeros((1, 128), F32)
        rate = jnp.zeros((1, 128), F32)
        for h in range(16):
            shift = jnp.where(side == h, step_bias[h], shift)
            rate = jnp.where(side == h, decay_log[h], rate)
        raw = dot(stepb[...], take) + shift
        dt = jnp.maximum(raw, 0.0) + jnp.log1p(jnp.exp(-jnp.abs(raw)))
        drop = dt * -jnp.exp(rate)
        ones = lower.astype(F32)
        for b in range(2):
            rows = slice(b * SPAN, (b + 1) * SPAN)
            cum = dot(ones, drop[rows], precision=lax.Precision.HIGHEST)
            cum_c[rows, :] = cum
            cum_r[b] = cum.T
            dt_r[b] = dt[rows].T
            if b == 0:
                w_c[...] = jnp.exp(cum[SPAN - 1 : SPAN] - cum) * dt[rows]

    def scan_inner():
        arrive(in_proj)
        for b in range(2):
            rows = slice(b * SPAN, (b + 1) * SPAN)
            inner[b] = dot(projb[rows, 256:512], projb[rows, 0:256], BT)
        arrive(in_x)

    def pair(hp, carry):
        cols = pl.ds(pl.multiple_of(hp * 128, 128), 128)
        skip = jnp.where(half, skip_gain[hp * 2], skip_gain[hp * 2 + 1])
        for b in range(2):
            rows = slice(b * SPAN, (b + 1) * SPAN)
            xp = xb[rows, cols]
            cum_b = cum_c[rows, :]
            res, cumcols, weights = [], [], []
            for e in range(2):
                h = hp * 2 + e
                column = pltpu.roll(cum_b, 128 - h, 1)[:, 0:1]
                spread_cum = column - cum_r[b, pl.ds(h, 1), :]
                mix = jnp.exp(jnp.where(lower, spread_cum, LOW)) * inner[b] * dt_r[b, pl.ds(h, 1), :]
                res.append(dot(mix.astype(BF16), xp))
                cumcols.append(column)
                if b == 0:
                    weights.append(pltpu.roll(w_c[...], 128 - h, 1)[:, 0:1])
            xf = xp.astype(F32)
            ecx[rows, cols] = jnp.exp(jnp.where(half, cumcols[0], cumcols[1]))
            yint[rows, cols] = jnp.where(half, res[0], res[1]) + skip * xf
            if b == 0:
                tailb[:, cols] = (jnp.where(half, weights[0], weights[1]) * xf).astype(BF16)
        return carry

    def scan_add():
        add_s[...] = dot(projb[0:SPAN, 0:256], tailb[...], AT)

    def open_gate():
        in_gate.wait()

        def some(g, carry):
            cols = pl.ds(pl.multiple_of(g * 1024, 1024), 1024)
            gv = gateb[:, cols].astype(F32)
            gact[:, cols] = gv / (1.0 + jnp.exp(-gv))
            return carry

        lax.fori_loop(0, NT, some, 0)

    ssm_sends = []

    def carry_in(lo, hi):
        e = entry[r]
        ze = lax.div(e, NY)
        behind = lax.rem(z - ze + NZ, NZ)
        eye = (
            lax.broadcasted_iota(jnp.int32, (256, 256), 0) == lax.broadcasted_iota(jnp.int32, (256, 256), 1)
        ).astype(BF16)
        for c in range(lo, hi):
            ahead, back = length(c % 2, 1), length(c % 2, -1)
            entering = jnp.where(behind <= ahead, tk[c][ahead - 1], tk[c][4 + back - 1])
            s0 = jnp.where(ze == z, yb[c][lax.rem(e, NY)], entering)
            cols = slice(c * 128, (c + 1) * 128)
            s0t = dot(eye, s0, BT)
            s1t = ecx[SPAN - 1 : SPAN, cols] * s0t + add_s[:, cols]
            for b, st in ((0, s0t), (1, s1t)):
                rows = slice(b * SPAN, (b + 1) * SPAN)
                carried = dot(projb[rows, 256:512], st.astype(BF16))
                osend[rows, cols] = (yint[rows, cols] + ecx[rows, cols] * carried).astype(BF16)
        cols = slice(lo * 128, hi * 128)
        for d in range(1, NT):
            to = tp_of(d)
            ssm_sends.append(
                start(
                    remote(
                        osend.at[pl.ds(pl.multiple_of(to * ROWS, ROWS), ROWS), cols],
                        ob.at[my_rows, cols],
                        oss.at[lo, d - 1],
                        osr.at[lo, d - 1],
                        (r, to),
                    )
                )
            )
        ob[my_rows, cols] = osend[my_rows, cols]

    def attend_fresh(i, carry):
        head = i // 2
        tile = lax.rem(i, 2)
        qt = qb[pl.ds(pl.multiple_of(tile * 256, 256), 256), pl.ds(pl.multiple_of(head * 128, 128), 128)]
        s = dot(qt, fb[:, 0:128], BT)
        allowed = lax.broadcasted_iota(jnp.int32, (256, 512), 1) <= (
            lax.broadcasted_iota(jnp.int32, (256, 512), 0) + tile * 256
        )
        s = jnp.where(allowed, s, LOW)
        top = jnp.max(s, axis=1, keepdims=True)
        w = jnp.exp2((s - top) * SCALE)
        m_s[i] = jnp.broadcast_to(top, (256, 128))
        l_s[i] = jnp.broadcast_to(jnp.sum(w, axis=1, keepdims=True), (256, 128))
        acc_s[i] = dot(w.astype(BF16), fb[:, 128:256])
        return carry

    def attend_first():
        arrive(in_q)
        arrive(in_f)
        lax.fori_loop(0, 8, attend_fresh, 0)

    def attend_cached(n, lo, hi):
        if lo == 0:
            for k in (2 * n, 2 * n + 1):
                for j in range(1, NY):
                    kv_copies[k, j].wait_recv()

        def tile_of(i, carry):
            head = i // 2
            tile = lax.rem(i, 2)
            qt = qb[
                pl.ds(pl.multiple_of(tile * 256, 256), 256), pl.ds(pl.multiple_of(head * 128, 128), 128)
            ]
            block = kvb[2 * n : 2 * n + 2].reshape(1024, 256)
            s = dot(qt, block[:, 0:128], BT) + bias[n]
            old = m_s[i][:, 0:1]
            top = jnp.maximum(old, jnp.max(s, axis=1, keepdims=True))
            w = jnp.exp2((s - top) * SCALE)
            fade = jnp.exp2((old - top) * SCALE)
            m_s[i] = jnp.broadcast_to(top, (256, 128))
            l_s[i] = l_s[i] * fade + jnp.sum(w, axis=1, keepdims=True)
            acc_s[i] = acc_s[i] * fade + dot(w.astype(BF16), block[:, 128:256])
            return carry

        lax.fori_loop(lo, hi, tile_of, 0)

    my_cols = pl.ds(pl.multiple_of(p * 512, 512), 512)
    attn_sends = []
    own_attn = []

    def finish(i, carry):
        head = i // 2
        tile = lax.rem(i, 2)
        alive = lax.broadcasted_iota(jnp.int32, (256, 128), 0) + tile * 256 < live
        value = jnp.where(alive, acc_s[i] / l_s[i], 0.0)
        ao[
            pl.ds(pl.multiple_of(tile * 256, 256), 256), pl.ds(pl.multiple_of(head * 128, 128), 128)
        ] = value.astype(BF16)
        return carry

    def attend_last():
        lax.fori_loop(0, 8, finish, 0)
        for d in range(1, NT):
            to = tp_of(d)
            attn_sends.append(
                start(
                    remote(
                        ao.at[pl.ds(pl.multiple_of(to * ROWS, ROWS), ROWS), :],
                        attn_out.at[:, my_cols],
                        aos.at[d - 1],
                        aor.at[d - 1],
                        (r, to),
                    )
                )
            )
        own_attn.append(start_local(ao.at[my_rows, :], attn_out.at[:, my_cols]))

    waiting = [("kv", 0), ("kv", 1)] + [("st", c) for c in range(PARTS)]
    under_way = []
    ended = []
    work = list(WORK)
    done = set()
    count_rounds = 0
    marks = []

    def do(item):
        name, args = item[1], item[2:]
        if name == "sums":
            scan_sums()
        elif name == "inner":
            scan_inner()
        elif name == "pair":
            lax.fori_loop(args[0], args[1], pair, 0)
        elif name == "carry":
            carry_in(*args)
        elif name == "fresh":
            attend_first()
        elif name == "cached":
            attend_cached(*args)
        elif name == "finish":
            attend_last()
        elif name == "add":
            scan_add()
        elif name == "gate":
            open_gate()
        elif name == "gain":
            arrive(in_gain)
        elif name == "drain":
            while pending[0] is not marks[args[0]]:
                pending.pop(0).wait_send()

    def able(item):
        if item[1] == "carry":
            return all(c in done for c in range(item[2], item[3]))
        return item[0] <= count_rounds

    while waiting or under_way:
        for one in list(under_way):
            kind, n, s = one
            (kv_step if kind == "kv" else tok_step)(n, s)
            if s == 4:
                under_way.remove(one)
                if kind == "st":
                    done.add(n)
            else:
                under_way[under_way.index(one)] = (kind, n, s + 1)
        room = 2 if count_rounds < 1 else 1
        while waiting and len(under_way) < FLIGHT and room > 0:
            room -= 1
            kind, n = waiting.pop(0)
            if kind == "st":
                tok_start(n)
            under_way.append((kind, n, 1))
        count_rounds += 1
        marks.append(pending[-1])
        budget = BUDGET
        for item in list(work):
            if budget > 0 and able(item):
                work.remove(item)
                do(item)
                budget -= COST[item[1]]
    for item in list(work):
        do(item)

    for copy in ssm_sends:
        copy.wait_recv()

    def norm(g, carry):
        rows = pl.ds(pl.multiple_of(g * ROWS, ROWS), ROWS)
        parts = []
        square = jnp.zeros((ROWS, 1), F32)
        for c in range(4):
            act = gact[:, pl.ds(pl.multiple_of(g * 1024 + c * 256, 256), 256)]
            gated = ob[rows, c * 256 : (c + 1) * 256].astype(F32) * act
            parts.append(gated)
            square = square + jnp.sum(gated * gated, axis=1, keepdims=True)
        factor = lax.rsqrt(square * (1.0 / 1024) + 1e-5)
        alive = lax.broadcasted_iota(jnp.int32, (ROWS, 1), 0) + p * ROWS < live
        factor = jnp.where(alive, factor, 0.0)
        gains = gainb[g]
        for c in range(4):
            for e in range(2):
                k = c * 2 + e
                ssm_out[:, pl.ds(pl.multiple_of(g * 1024 + k * 128, 128), 128)] = (
                    parts[c][:, e * 128 : (e + 1) * 128] * factor * gains[k : k + 1, :]
                ).astype(BF16)
        return carry

    lax.fori_loop(0, NT, norm, 0)

    own_attn[0].wait()
    for copy in attn_sends:
        copy.wait_recv()
    for copy in pending:
        copy.wait_send()


BUDGET = 3.5
COST = {
    "sums": 1.0,
    "inner": 0.5,
    "pair": 1.5,
    "add": 0.6,
    "carry": 1.2,
    "fresh": 4.0,
    "cached": 1.6,
    "finish": 1.0,
    "gate": 1.2,
    "gain": 0.1,
    "drain": 0.3,
}
WORK = (
    (3, "sums"),
    (3, "gate"),
    (4, "inner"),
    (4, "pair", 0, 2),
    (4, "pair", 2, 4),
    (5, "pair", 4, 6),
    (5, "pair", 6, 8),
    (5, "add"),
    (6, "carry", 0, 2),
    (6, "gain"),
    (6, "fresh"),
    (6, "carry", 2, 4),
    (7, "drain", 1),
    (7, "cached", 0, 0, 2),
    (7, "cached", 0, 2, 4),
    (7, "cached", 0, 4, 6),
    (7, "cached", 0, 6, 8),
    (8, "carry", 4, 6),
    (8, "cached", 1, 0, 2),
    (8, "cached", 1, 2, 4),
    (8, "cached", 1, 4, 6),
    (8, "cached", 1, 6, 8),
    (9, "drain", 4),
    (9, "cached", 2, 0, 2),
    (9, "cached", 2, 2, 4),
    (9, "cached", 2, 4, 6),
    (9, "cached", 2, 6, 8),
    (10, "cached", 3, 0, 2),
    (10, "cached", 3, 2, 4),
    (10, "cached", 3, 4, 6),
    (10, "cached", 3, 6, 8),
    (10, "finish"),
    (11, "drain", 8),
    (12, "carry", 6, 7),
    (12, "carry", 7, 8),
)


def run(*args):
    any_ = pl.BlockSpec(memory_space=pl.ANY)
    vmem = pl.BlockSpec(memory_space=pltpu.VMEM)
    dma = pltpu.SemaphoreType.DMA
    return pl.pallas_call(
        kernel,
        out_shape=(
            jax.ShapeDtypeStruct((ROWS, 8192), BF16),
            jax.ShapeDtypeStruct((ROWS, 4096), BF16),
        ),
        in_specs=[any_] * 17,
        out_specs=(vmem, any_),
        scratch_shapes=[
            pltpu.VMEM((NZ * NY, 64), jnp.int32),
            pltpu.VMEM((NZ * NY, 64), jnp.int32),
            pltpu.SMEM((NZ * NY,), jnp.int32),
            pltpu.SMEM((NZ * NY,), jnp.int32),
            pltpu.SMEM((NZ * NY,), jnp.int32),
            pltpu.SMEM((16,), F32),
            pltpu.SMEM((16,), F32),
            pltpu.SMEM((16,), F32),
            pltpu.VMEM((NZ * NY, 128), jnp.int32),
            pltpu.SMEM((NZ * NY, 128), jnp.int32),
            pltpu.VMEM((4, 1, 1024), F32),
            pltpu.VMEM((512, 128), BF16),
            pltpu.VMEM((NT, 8, 128), F32),
            pltpu.VMEM((512, 512), BF16),
            pltpu.VMEM((512, 1024), BF16),
            pltpu.VMEM((512, 512), BF16),
            pltpu.VMEM((512, 256), BF16),
            pltpu.VMEM((ROWS, 8192), BF16),
            pltpu.VMEM((ROWS, 8192), F32),
            pltpu.VMEM((256, 1024), F32),
            [pltpu.VMEM((4, 64, 256), BF16)] * 8,
            pltpu.VMEM((8, 3, 2, 64, 256), BF16),
            pltpu.VMEM((8, NY, 2, 64, 256), BF16),
            [pltpu.VMEM((NY, 128, 256), BF16)] * PARTS,
            [pltpu.VMEM((8, 128, 256), BF16)] * PARTS,
            [pltpu.VMEM((8, 128, 256), BF16)] * PARTS,
            pltpu.VMEM((512, 128), F32),
            pltpu.VMEM((256, 128), F32),
            pltpu.VMEM((2, 128, 256), F32),
            pltpu.VMEM((2, 128, 256), F32),
            pltpu.VMEM((2, 256, 256), F32),
            pltpu.VMEM((512, 1024), F32),
            pltpu.VMEM((512, 1024), F32),
            pltpu.VMEM((256, 1024), BF16),
            pltpu.VMEM((512, 1024), BF16),
            pltpu.VMEM((512, 1024), BF16),
            pltpu.VMEM((8, 256, 128), F32),
            pltpu.VMEM((8, 256, 128), F32),
            pltpu.VMEM((8, 256, 128), F32),
            pltpu.VMEM((512, 512), BF16),
            dma((9,)),
            dma((24,)),
            dma((6, 7)),
            dma((6, 7)),
            dma((2, 8)),
            dma((2, 8)),
            dma((8, 3)),
            dma((8, 3)),
            dma((PARTS, 3)),
            dma((PARTS, 3)),
            dma((PARTS, 8)),
            dma((PARTS, 8)),
            dma((PARTS, 7)),
            dma((PARTS, 7)),
            dma((7,)),
            dma((7,)),
        ],
        compiler_params=pltpu.CompilerParams(
            collective_id=0, has_side_effects=True, vmem_limit_bytes=56 * 2**20
        ),
        name="prefill",
    )(*args)


def per_device(
    ssm_input,
    ssm_gate,
    state_proj,
    step_raw,
    queries,
    fresh_kv,
    block_pool,
    state_pool,
    decay_log,
    step_bias,
    skip_gain,
    norm_gain,
    block_owner,
    block_slot,
    block_count,
    state_entry,
    suffix_len,
):
    ssm, attn = run(
        block_owner,
        block_slot,
        block_count,
        state_entry,
        suffix_len,
        decay_log,
        step_bias,
        skip_gain,
        norm_gain.reshape(8, 128),
        step_raw[0],
        state_proj[0],
        ssm_input[0],
        queries[0],
        fresh_kv[0],
        ssm_gate[0],
        block_pool.reshape(4, 64, 256),
        state_pool.reshape(PARTS, 128, 256),
    )
    return (ssm[None], attn[None])


def solution(mesh):
    return jax.shard_map(
        per_device,
        mesh=mesh,
        in_specs=(
            P("req", "tp", None),
            P("req", "tp", None),
            P("req", "tp", None),
            P("req", "tp", None),
            P("req", "tp", None),
            P("req", "tp", None),
            P("req", None, "tp", None),
            P("req", "tp", None, None),
            P("tp"),
            P("tp"),
            P("tp"),
            P("tp"),
            P(),
            P(),
            P(),
            P(),
            P(),
        ),
        out_specs=(P("req", "tp", None), P("req", "tp", None)),
        check_vma=False,
    )
```

```python
import jax
import jax.numpy as jnp
from jax import lax
from jax.experimental import pallas as pl
from jax.experimental.pallas import tpu as pltpu
from jax.sharding import PartitionSpec as P

MESH = pl.DeviceIdType.MESH
F32 = jnp.float32
BF16 = jnp.bfloat16

NZ, NY, NT = 8, 4, 8
ROWS = 64
SPAN = 256
PARTS = 8
FLIGHT = 6
DIST = (0, 1, -1, 2, -2, 3, -3, 4)
LOW = -1e30
SCALE = 1.4426950408889634 / 128**0.5


def dot(a, b, dims=(((1,), (0,)), ((), ())), precision=None):
    return lax.dot_general(a, b, dims, precision=precision, preferred_element_type=F32)


BT = (((1,), (1,)), ((), ()))
AT = (((0,), (0,)), ((), ()))


def kernel(
    owner_in,
    slot_in,
    count_in,
    entry_in,
    suffix_in,
    decay_in,
    bias_in,
    skip_in,
    gain,
    step,
    proj,
    xin,
    query,
    fresh,
    gate,
    pool,
    state,
    ssm_out,
    attn_out,
    owner,
    slot,
    count,
    entry,
    suffix,
    decay_log,
    step_bias,
    skip_gain,
    tabv,
    tabs,
    stepb,
    gainb,
    projb,
    xb,
    qb,
    fb,
    gateb,
    gact,
    add_s,
    kz,
    ksend,
    kvb,
    yb,
    tk,
    ts,
    cum_c,
    w_c,
    cum_r,
    dt_r,
    inner,
    yint,
    ecx,
    tailb,
    osend,
    ob,
    q2,
    kk,
    vt,
    m_s,
    acc_s,
    ao,
    tsem,
    lsem,
    xs,
    xr,
    kzs,
    kzr,
    kys,
    kyr,
    sys_,
    syr,
    tss,
    tsr,
    oss,
    osr,
    aos,
    aor,
):
    r = lax.axis_index("req")
    p = lax.axis_index("tp")
    z = r // NY
    y = lax.rem(r, NY)

    def tp_of(d):
        return lax.rem(p + d, NT)

    def z_of(k):
        return lax.rem(z + k + 2 * NZ, NZ)

    def y_of(k):
        return lax.rem(y + k + NY, NY)

    def remote(src, dst, ssem, rsem, device):
        return pltpu.make_async_remote_copy(
            src_ref=src, dst_ref=dst, send_sem=ssem, recv_sem=rsem, device_id=device, device_id_type=MESH
        )

    small = [
        pltpu.make_async_copy(src, dst, tsem.at[1 + i])
        for i, (src, dst) in enumerate(
            (
                (owner_in, owner),
                (slot_in, slot),
                (count_in, count),
                (entry_in, entry),
                (suffix_in, suffix),
                (decay_in, decay_log),
                (bias_in, step_bias),
                (skip_in, skip_gain),
            )
        )
    ]
    for copy in small:
        copy.start()

    barrier = pltpu.get_barrier_semaphore()
    peers = [(r, tp_of(d)) for d in range(1, NT)]
    peers += [(z_of(1) * NY + y, p), (z_of(-1) * NY + y, p)]
    peers += [(z * NY + y_of(j), p) for j in range(1, NY)]
    for peer in peers:
        pl.semaphore_signal(barrier, inc=1, device_id=peer, device_id_type=MESH)

    pending = []
    local = []

    def start(copy):
        copy.start()
        pending.append(copy)
        return copy

    def start_local(src, dst):
        copy = pltpu.make_async_copy(src, dst, lsem.at[len(local)])
        copy.start()
        local.append(copy)
        return copy

    my_rows = pl.ds(pl.multiple_of(p * ROWS, ROWS), ROWS)
    own_pool = start_local(pool, kz[0])

    pl.semaphore_wait(barrier, len(peers))

    def spread(i, src, dst, width):
        out = [start_local(src.at[:, pl.ds(pl.multiple_of(p * width, 128), width)], dst.at[my_rows, :])]
        for d in range(1, NT):
            to = tp_of(d)
            out.append(
                start(
                    remote(
                        src.at[:, pl.ds(pl.multiple_of(to * width, 128), width)],
                        dst.at[my_rows, :],
                        xs.at[i, d - 1],
                        xr.at[i, d - 1],
                        (r, to),
                    )
                )
            )
        return out

    def everyone(i, src, dst):
        out = [start_local(src, dst)]
        for d in range(1, NT):
            out.append(start(remote(src, dst, xs.at[i, d - 1], xr.at[i, d - 1], (r, tp_of(d)))))
        return out

    def arrive(copies):
        copies[0].wait()
        for copy in copies[1:]:
            copy.wait_recv()

    gathers = {}

    def gather_state(c):
        out = [start_local(state.at[c], yb[c].at[y])]
        for j in range(1, NY):
            out.append(
                start(
                    remote(
                        state.at[c],
                        yb[c].at[y],
                        sys_.at[c, j - 1],
                        syr.at[c, j - 1],
                        (z * NY + y_of(j), p),
                    )
                )
            )
        gathers[c] = out

    def length(parity, way):
        return 4 if (way > 0) == (parity == 0) else 3

    hops = {}

    def kv_slot(s, way):
        return DIST.index(s * way) if s < 4 else 7

    def kv_hop(f, s, way):
        slot_now = kv_slot(s, way)
        part = pl.ds(2 * f, 2)
        before = pool if s == 1 else kz[kv_slot(s - 1, way)]
        place = slot_now
        hops[f, s, way] = start(
            remote(
                before.at[part],
                kz[place].at[part],
                kzs.at[f, place],
                kzr.at[f, place],
                (z_of(way) * NY + y, p),
            )
        )

    kv_copies = {}

    def kv_across(k):
        source = lax.rem(z - DIST[k] + NZ, NZ) * NY + y
        for j in range(NY):
            to = y_of(j)
            word = tabs[source, to]
            first = kz[k][lax.rem(word, 4)]
            second = kz[k][lax.rem(lax.div(word, 4), 4)]
            if j == 0:
                kvb[k, y, 0] = first
                kvb[k, y, 1] = second
            else:
                ksend[k, j - 1, 0] = first
                ksend[k, j - 1, 1] = second
                kv_copies[k, j] = start(
                    remote(
                        ksend.at[k, j - 1],
                        kvb.at[k, y],
                        kys.at[k, j - 1],
                        kyr.at[k, j - 1],
                        (z * NY + to, p),
                    )
                )

    def kv_step(f, s):
        for way in (1, -1):
            if s <= length(f, way):
                hops[f, s, way].wait_recv()
                if s < length(f, way):
                    kv_hop(f, s + 1, way)
        if f == 1:
            if s < 4:
                kv_across(DIST.index(s))
                kv_across(DIST.index(-s))
            else:
                kv_across(7)

    tokens = {}

    def tok_hop(c, s, way):
        total = length(c % 2, way)
        dest = z_of(way * (total - s + 1))
        base = 0 if way > 0 else 4
        e = entry[dest * NY + y]
        mine = yb[c][lax.rem(e, NY)]
        if s > 1:
            mine = jnp.where(lax.div(e, NY) == z, mine, tk[c][base + s - 2])
        ts[c][base + s - 1] = mine
        tokens[c, s, way] = start(
            remote(
                ts[c].at[base + s - 1],
                tk[c].at[base + s - 1],
                tss.at[c, base + s - 1],
                tsr.at[c, base + s - 1],
                (z_of(way) * NY + y, p),
            )
        )

    def tok_start(c):
        arrive(gathers[c])
        tok_hop(c, 1, 1)
        tok_hop(c, 1, -1)

    def tok_step(c, s):
        for way in (1, -1):
            if s <= length(c % 2, way):
                tokens[c, s, way].wait_recv()
                if s < length(c % 2, way):
                    tok_hop(c, s + 1, way)

    for f in range(2):
        kv_hop(f, 1, 1)
        kv_hop(f, 1, -1)
    gather_state(0)
    gather_state(1)
    arrays = {}

    def leave(name):
        if name == "step":
            arrays[name] = everyone(0, step, stepb.at[my_rows, :])
        elif name == "proj":
            arrays[name] = spread(1, proj, projb, 512)
        elif name == "x":
            arrays[name] = spread(2, xin, xb, 1024)
        elif name == "q":
            arrays[name] = spread(3, query, qb, 512)
        elif name == "f":
            arrays[name] = spread(4, fresh, fb, 256)
        elif name == "gain":
            arrays[name] = everyone(5, gain, gainb.at[p])
        elif name == "gate":
            arrays[name] = start_local(gate, gateb)

    leave("step")

    for copy in small:
        copy.wait()
    lane = lax.broadcasted_iota(jnp.int32, (NZ * NY, 64), 1)
    who = lax.broadcasted_iota(jnp.int32, (NZ * NY, 64), 0)
    wide = lax.broadcasted_iota(jnp.int32, (NZ * NY, 128), 1)
    packed = jnp.zeros((NZ * NY, 128), jnp.int32)
    for t in range(NY):
        row = pl.ds(z * NY + t, 1)
        named = (owner[row, :] == who) & (lane < count[z * NY + t])
        code = lane * 4 + slot[row, :]
        first = jnp.min(jnp.where(named, code, 1024), axis=1, keepdims=True)
        last = jnp.max(jnp.where(named, code, -1), axis=1, keepdims=True)
        value = (
            (first & 3)
            + 4 * (last & 3)
            + jnp.where(first < 1024, 16, 0)
            + jnp.where(last > first, 32, 0)
        )
        packed = jnp.where(wide == t, value, packed)
    tabv[...] = packed
    to_scalars = pltpu.make_async_copy(tabv, tabs, tsem.at[0])
    to_scalars.start()

    to_scalars.wait()
    own_pool.wait()
    kv_across(0)
    live = suffix[r]

    side = lax.broadcasted_iota(jnp.int32, (1, 128), 1)

    lower = lax.broadcasted_iota(jnp.int32, (SPAN, SPAN), 0) >= lax.broadcasted_iota(
        jnp.int32, (SPAN, SPAN), 1
    )
    half = lax.broadcasted_iota(jnp.int32, (SPAN, 128), 1) < 64

    def scan_sums():
        arrive(arrays["step"])
        take = (
            lax.broadcasted_iota(jnp.int32, (128, 128), 0)
            == lax.broadcasted_iota(jnp.int32, (128, 128), 1) + p * 16
        ).astype(BF16)
        shift = jnp.zeros((1, 128), F32)
        rate = jnp.zeros((1, 128), F32)
        for h in range(16):
            shift = jnp.where(side == h, step_bias[h], shift)
            rate = jnp.where(side == h, decay_log[h], rate)
        raw = dot(stepb[...], take) + shift
        dt = jnp.maximum(raw, 0.0) + jnp.log1p(jnp.exp(-jnp.abs(raw)))
        drop = dt * -jnp.exp(rate)
        ones = lower.astype(F32)
        for b in range(2):
            rows = slice(b * SPAN, (b + 1) * SPAN)
            cum = dot(ones, drop[rows], precision=lax.Precision.HIGHEST)
            cum_c[rows, :] = cum
            cum_r[b] = cum.T
            dt_r[b] = dt[rows].T
            if b == 0:
                w_c[...] = jnp.exp(cum[SPAN - 1 : SPAN] - cum) * dt[rows]

    def scan_inner():
        arrive(arrays["proj"])
        for b in range(2):
            rows = slice(b * SPAN, (b + 1) * SPAN)
            inner[b] = dot(projb[rows, 256:512], projb[rows, 0:256], BT)
        arrive(arrays["x"])

    def pair(hp, carry):
        cols = pl.ds(pl.multiple_of(hp * 128, 128), 128)
        skip = jnp.where(half, skip_gain[hp * 2], skip_gain[hp * 2 + 1])
        for b in range(2):
            rows = slice(b * SPAN, (b + 1) * SPAN)
            xp = xb[rows, cols]
            cum_b = cum_c[rows, :]
            res, cumcols, weights = [], [], []
            for e in range(2):
                h = hp * 2 + e
                column = pltpu.roll(cum_b, 128 - h, 1)[:, 0:1]
                spread_cum = column - cum_r[b, pl.ds(h, 1), :]
                mix = jnp.exp(jnp.where(lower, spread_cum, LOW)) * inner[b] * dt_r[b, pl.ds(h, 1), :]
                res.append(dot(mix.astype(BF16), xp))
                cumcols.append(column)
                if b == 0:
                    weights.append(pltpu.roll(w_c[...], 128 - h, 1)[:, 0:1])
            xf = xp.astype(F32)
            ecx[rows, cols] = jnp.exp(jnp.where(half, cumcols[0], cumcols[1]))
            yint[rows, cols] = jnp.where(half, res[0], res[1]) + skip * xf
            if b == 0:
                tailb[:, cols] = (jnp.where(half, weights[0], weights[1]) * xf).astype(BF16)
        return carry

    def scan_add():
        add_s[...] = dot(projb[0:SPAN, 0:256], tailb[...], AT)

    def open_gate():
        arrays["gate"].wait()

        def some(g, carry):
            cols = pl.ds(pl.multiple_of(g * 1024, 1024), 1024)
            gv = gateb[:, cols].astype(F32)
            gact[:, cols] = gv / (1.0 + jnp.exp(-gv))
            return carry

        lax.fori_loop(0, NT, some, 0)

    ssm_sends = []

    def carry_in(lo, hi):
        e = entry[r]
        ze = lax.div(e, NY)
        behind = lax.rem(z - ze + NZ, NZ)
        eye = (
            lax.broadcasted_iota(jnp.int32, (256, 256), 0) == lax.broadcasted_iota(jnp.int32, (256, 256), 1)
        ).astype(BF16)
        for c in range(lo, hi):
            ahead, back = length(c % 2, 1), length(c % 2, -1)
            entering = jnp.where(behind <= ahead, tk[c][ahead - 1], tk[c][4 + back - 1])
            s0 = jnp.where(ze == z, yb[c][lax.rem(e, NY)], entering)
            cols = slice(c * 128, (c + 1) * 128)
            s0t = dot(eye, s0, BT)
            s1t = ecx[SPAN - 1 : SPAN, cols] * s0t + add_s[:, cols]
            for b, st in ((0, s0t), (1, s1t)):
                rows = slice(b * SPAN, (b + 1) * SPAN)
                carried = dot(projb[rows, 256:512], st.astype(BF16))
                osend[rows, cols] = (yint[rows, cols] + ecx[rows, cols] * carried).astype(BF16)
        cols = slice(lo * 128, hi * 128)
        for d in range(1, NT):
            to = tp_of(d)
            ssm_sends.append(
                start(
                    remote(
                        osend.at[pl.ds(pl.multiple_of(to * ROWS, ROWS), ROWS), cols],
                        ob.at[my_rows, cols],
                        oss.at[lo, d - 1],
                        osr.at[lo, d - 1],
                        (r, to),
                    )
                )
            )
        ob[my_rows, cols] = osend[my_rows, cols]

    def set_block(block, rows):
        kk[0:rows, 0:128] = block[:, 0:128]
        kk[0:rows, 128:256] = block[:, 0:128]
        vt[0:128, 0:rows] = block[:, 128:256].T

    def attend_first():
        arrive(arrays["q"])
        arrive(arrays["f"])
        for head in range(4):
            qf = qb[:, head * 128 : (head + 1) * 128].astype(F32) * SCALE
            high = qf.astype(BF16)
            q2[head, :, 0:128] = high
            q2[head, :, 128:256] = (qf - high.astype(F32)).astype(BF16)
        vt[128:144, :] = jnp.ones((16, 1024), BF16)
        set_block(fb[...], 512)
        allowed = lax.broadcasted_iota(jnp.int32, (512, 512), 0) <= lax.broadcasted_iota(
            jnp.int32, (512, 512), 1
        )
        for head in range(4):
            s = jnp.where(allowed, dot(kk[0:512, :], q2[head], BT), LOW)
            top = jnp.max(s, axis=0, keepdims=True)
            w = jnp.exp2(s - top).astype(BF16)
            m_s[head] = jnp.broadcast_to(top, (8, 512))
            acc_s[head] = dot(vt[:, 0:512], w)

    def attend_cached(n, part):
        if part == 0:
            for k in (2 * n, 2 * n + 1):
                for j in range(1, NY):
                    kv_copies[k, j].wait_recv()
            set_block(kvb[2 * n : 2 * n + 2].reshape(1024, 256), 1024)
        blocked = []
        for k in (2 * n, 2 * n + 1):
            for t in range(NY):
                word = tabs[lax.rem(z - DIST[k] + NZ, NZ) * NY + t, y]
                blocked.append(jnp.where(lax.rem(lax.div(word, 16), 2) > 0, 0.0, LOW))
                blocked.append(jnp.where(lax.div(word, 32) > 0, 0.0, LOW))
        for head in (2 * part, 2 * part + 1):
            s = dot(kk[...], q2[head], BT)
            s = jnp.concatenate([s[b * 64 : (b + 1) * 64] + blocked[b] for b in range(16)], axis=0)
            old = m_s[head][0:1, :]
            top = jnp.maximum(old, jnp.max(s, axis=0, keepdims=True))
            w = jnp.exp2(s - top).astype(BF16)
            m_s[head] = jnp.broadcast_to(top, (8, 512))
            acc_s[head] = acc_s[head] * jnp.exp2(old - top) + dot(vt[...], w)

    my_cols = pl.ds(pl.multiple_of(p * 512, 512), 512)
    attn_sends = []
    own_attn = []

    def attend_last():
        alive = lax.broadcasted_iota(jnp.int32, (128, 512), 1) < live
        for head in range(4):
            value = jnp.where(alive, acc_s[head, 0:128] / acc_s[head, 128:129], 0.0)
            ao[:, head * 128 : (head + 1) * 128] = value.T.astype(BF16)
        for d in range(1, NT):
            to = tp_of(d)
            attn_sends.append(
                start(
                    remote(
                        ao.at[pl.ds(pl.multiple_of(to * ROWS, ROWS), ROWS), :],
                        attn_out.at[:, my_cols],
                        aos.at[d - 1],
                        aor.at[d - 1],
                        (r, to),
                    )
                )
            )
        own_attn.append(start_local(ao.at[my_rows, :], attn_out.at[:, my_cols]))

    waiting = [("kv", 0), ("kv", 1)] + [("st", c) for c in range(PARTS)]
    under_way = []
    ended = []
    work = list(WORK)
    done = set()
    count_rounds = 0
    marks = []

    def do(item):
        name, args = item[1], item[2:]
        if name == "sums":
            scan_sums()
        elif name == "inner":
            scan_inner()
        elif name == "pair":
            lax.fori_loop(args[0], args[1], pair, 0)
        elif name == "carry":
            carry_in(*args)
        elif name == "fresh":
            attend_first()
        elif name == "cached":
            attend_cached(*args)
        elif name == "finish":
            attend_last()
        elif name == "leave":
            leave(*args)
        elif name == "gather":
            for c in range(*args):
                gather_state(c)
        elif name == "add":
            scan_add()
        elif name == "gate":
            open_gate()
        elif name == "gain":
            arrive(arrays["gain"])
        elif name == "drain":
            while pending[0] is not marks[args[0]]:
                pending.pop(0).wait_send()

    def able(item):
        if item[1] == "carry":
            return all(c in done for c in range(item[2], item[3]))
        return item[0] <= count_rounds

    while waiting or under_way:
        for one in list(under_way):
            kind, n, s = one
            (kv_step if kind == "kv" else tok_step)(n, s)
            if s == 4:
                under_way.remove(one)
                if kind == "st":
                    done.add(n)
            else:
                under_way[under_way.index(one)] = (kind, n, s + 1)
        room = 2 if count_rounds < 1 else 1
        while waiting and len(under_way) < FLIGHT and room > 0:
            room -= 1
            kind, n = waiting.pop(0)
            if kind == "st":
                tok_start(n)
            under_way.append((kind, n, 1))
        count_rounds += 1
        marks.append(pending[-1])
        budget = BUDGET
        for item in list(work):
            if budget > 0 and able(item):
                work.remove(item)
                do(item)
                budget -= COST[item[1]]
    for item in list(work):
        do(item)

    for copy in ssm_sends:
        copy.wait_recv()

    def norm(g, carry):
        rows = pl.ds(pl.multiple_of(g * ROWS, ROWS), ROWS)
        parts = []
        square = jnp.zeros((ROWS, 1), F32)
        for c in range(4):
            act = gact[:, pl.ds(pl.multiple_of(g * 1024 + c * 256, 256), 256)]
            gated = ob[rows, c * 256 : (c + 1) * 256].astype(F32) * act
            parts.append(gated)
            square = square + jnp.sum(gated * gated, axis=1, keepdims=True)
        factor = lax.rsqrt(square * (1.0 / 1024) + 1e-5)
        alive = lax.broadcasted_iota(jnp.int32, (ROWS, 1), 0) + p * ROWS < live
        factor = jnp.where(alive, factor, 0.0)
        gains = gainb[g]
        for c in range(4):
            for e in range(2):
                k = c * 2 + e
                ssm_out[:, pl.ds(pl.multiple_of(g * 1024 + k * 128, 128), 128)] = (
                    parts[c][:, e * 128 : (e + 1) * 128] * factor * gains[k : k + 1, :]
                ).astype(BF16)
        return carry

    lax.fori_loop(0, NT, norm, 0)

    own_attn[0].wait()
    for copy in attn_sends:
        copy.wait_recv()
    for copy in pending:
        copy.wait_send()


BUDGET = 4.5
COST = {
    "leave": 0.5,
    "gather": 0.4,
    "sums": 1.0,
    "inner": 0.5,
    "pair": 1.5,
    "add": 0.6,
    "carry": 1.2,
    "fresh": 2.5,
    "cached": 2.0,
    "finish": 1.0,
    "gate": 1.2,
    "gain": 0.1,
    "drain": 0.3,
}
WORK = (
    (1, "leave", "proj"),
    (1, "leave", "x"),
    (1, "gather", 2, 4),
    (2, "gather", 4, 6),
    (2, "leave", "q"),
    (2, "leave", "f"),
    (3, "gather", 6, 8),
    (3, "leave", "gain"),
    (3, "leave", "gate"),
    (3, "sums"),
    (4, "gate"),
    (4, "inner"),
    (4, "pair", 0, 2),
    (4, "pair", 2, 4),
    (5, "pair", 4, 6),
    (5, "pair", 6, 8),
    (5, "add"),
    (6, "carry", 0, 2),
    (6, "gain"),
    (6, "fresh"),
    (6, "carry", 2, 4),
    (7, "drain", 1),
    (7, "cached", 0, 0),
    (7, "cached", 0, 1),
    (8, "carry", 4, 6),
    (8, "cached", 1, 0),
    (8, "cached", 1, 1),
    (9, "drain", 4),
    (9, "cached", 2, 0),
    (9, "cached", 2, 1),
    (10, "cached", 3, 0),
    (10, "cached", 3, 1),
    (10, "finish"),
    (11, "drain", 8),
    (12, "carry", 6, 7),
    (12, "carry", 7, 8),
)


def run(*args):
    any_ = pl.BlockSpec(memory_space=pl.ANY)
    vmem = pl.BlockSpec(memory_space=pltpu.VMEM)
    dma = pltpu.SemaphoreType.DMA
    return pl.pallas_call(
        kernel,
        out_shape=(
            jax.ShapeDtypeStruct((ROWS, 8192), BF16),
            jax.ShapeDtypeStruct((ROWS, 4096), BF16),
        ),
        in_specs=[any_] * 17,
        out_specs=(vmem, any_),
        scratch_shapes=[
            pltpu.VMEM((NZ * NY, 64), jnp.int32),
            pltpu.VMEM((NZ * NY, 64), jnp.int32),
            pltpu.SMEM((NZ * NY,), jnp.int32),
            pltpu.SMEM((NZ * NY,), jnp.int32),
            pltpu.SMEM((NZ * NY,), jnp.int32),
            pltpu.SMEM((16,), F32),
            pltpu.SMEM((16,), F32),
            pltpu.SMEM((16,), F32),
            pltpu.VMEM((NZ * NY, 128), jnp.int32),
            pltpu.SMEM((NZ * NY, 128), jnp.int32),
            pltpu.VMEM((512, 128), BF16),
            pltpu.VMEM((NT, 8, 128), F32),
            pltpu.VMEM((512, 512), BF16),
            pltpu.VMEM((512, 1024), BF16),
            pltpu.VMEM((512, 512), BF16),
            pltpu.VMEM((512, 256), BF16),
            pltpu.VMEM((ROWS, 8192), BF16),
            pltpu.VMEM((ROWS, 8192), F32),
            pltpu.VMEM((256, 1024), F32),
            [pltpu.VMEM((4, 64, 256), BF16)] * 8,
            pltpu.VMEM((8, 3, 2, 64, 256), BF16),
            pltpu.VMEM((8, NY, 2, 64, 256), BF16),
            [pltpu.VMEM((NY, 128, 256), BF16)] * PARTS,
            [pltpu.VMEM((8, 128, 256), BF16)] * PARTS,
            [pltpu.VMEM((8, 128, 256), BF16)] * PARTS,
            pltpu.VMEM((512, 128), F32),
            pltpu.VMEM((256, 128), F32),
            pltpu.VMEM((2, 128, 256), F32),
            pltpu.VMEM((2, 128, 256), F32),
            pltpu.VMEM((2, 256, 256), F32),
            pltpu.VMEM((512, 1024), F32),
            pltpu.VMEM((512, 1024), F32),
            pltpu.VMEM((256, 1024), BF16),
            pltpu.VMEM((512, 1024), BF16),
            pltpu.VMEM((512, 1024), BF16),
            pltpu.VMEM((4, 512, 256), BF16),
            pltpu.VMEM((1024, 256), BF16),
            pltpu.VMEM((144, 1024), BF16),
            pltpu.VMEM((4, 8, 512), F32),
            pltpu.VMEM((4, 144, 512), F32),
            pltpu.VMEM((512, 512), BF16),
            dma((9,)),
            dma((24,)),
            dma((6, 7)),
            dma((6, 7)),
            dma((2, 8)),
            dma((2, 8)),
            dma((8, 3)),
            dma((8, 3)),
            dma((PARTS, 3)),
            dma((PARTS, 3)),
            dma((PARTS, 8)),
            dma((PARTS, 8)),
            dma((PARTS, 7)),
            dma((PARTS, 7)),
            dma((7,)),
            dma((7,)),
        ],
        compiler_params=pltpu.CompilerParams(
            collective_id=0, has_side_effects=True, vmem_limit_bytes=56 * 2**20
        ),
        name="prefill",
    )(*args)


def per_device(
    ssm_input,
    ssm_gate,
    state_proj,
    step_raw,
    queries,
    fresh_kv,
    block_pool,
    state_pool,
    decay_log,
    step_bias,
    skip_gain,
    norm_gain,
    block_owner,
    block_slot,
    block_count,
    state_entry,
    suffix_len,
):
    ssm, attn = run(
        block_owner,
        block_slot,
        block_count,
        state_entry,
        suffix_len,
        decay_log,
        step_bias,
        skip_gain,
        norm_gain.reshape(8, 128),
        step_raw[0],
        state_proj[0],
        ssm_input[0],
        queries[0],
        fresh_kv[0],
        ssm_gate[0],
        block_pool.reshape(4, 64, 256),
        state_pool.reshape(PARTS, 128, 256),
    )
    return (ssm[None], attn[None])


def solution(mesh):
    return jax.shard_map(
        per_device,
        mesh=mesh,
        in_specs=(
            P("req", "tp", None),
            P("req", "tp", None),
            P("req", "tp", None),
            P("req", "tp", None),
            P("req", "tp", None),
            P("req", "tp", None),
            P("req", None, "tp", None),
            P("req", "tp", None, None),
            P("tp"),
            P("tp"),
            P("tp"),
            P("tp"),
            P(),
            P(),
            P(),
            P(),
            P(),
        ),
        out_specs=(P("req", "tp", None), P("req", "tp", None)),
        check_vma=False,
    )
```

```python
import jax
import jax.numpy as jnp
from jax import lax
from jax.experimental import pallas as pl
from jax.experimental.pallas import tpu as pltpu
from jax.sharding import PartitionSpec as P

MESH = pl.DeviceIdType.MESH
F32 = jnp.float32
BF16 = jnp.bfloat16

NZ, NY, NT = 8, 4, 8
ROWS = 64
SPAN = 256
PARTS = 8
FLIGHT = 6
DIST = (0, 1, -1, 2, -2, 3, -3, 4)
LOW = -1e30
SCALE = 1.4426950408889634 / 128**0.5


def dot(a, b, dims=(((1,), (0,)), ((), ())), precision=None):
    return lax.dot_general(a, b, dims, precision=precision, preferred_element_type=F32)


BT = (((1,), (1,)), ((), ()))
AT = (((0,), (0,)), ((), ()))


def kernel(
    owner_in,
    slot_in,
    count_in,
    entry_in,
    suffix_in,
    decay_in,
    bias_in,
    skip_in,
    gain,
    step,
    proj,
    xin,
    query,
    fresh,
    gate,
    pool,
    state,
    ssm_out,
    attn_out,
    owner,
    slot,
    count,
    entry,
    suffix,
    decay_log,
    step_bias,
    skip_gain,
    tabv,
    tabs,
    stepb,
    gainb,
    projb,
    xb,
    qb,
    fb,
    gateb,
    gact,
    add_s,
    kz,
    ksend,
    kvb,
    yb,
    tk,
    ts,
    cum_c,
    w_c,
    cum_r,
    dt_r,
    inner,
    yint,
    ecx,
    tailb,
    osend,
    ob,
    q2,
    kk,
    vt,
    m_s,
    acc_s,
    ao,
    tsem,
    lsem,
    xs,
    xr,
    kzs,
    kzr,
    kys,
    kyr,
    sys_,
    syr,
    tss,
    tsr,
    oss,
    osr,
    aos,
    aor,
):
    r = lax.axis_index("req")
    p = lax.axis_index("tp")
    z = r // NY
    y = lax.rem(r, NY)

    def tp_of(d):
        return lax.rem(p + d, NT)

    def z_of(k):
        return lax.rem(z + k + 2 * NZ, NZ)

    def y_of(k):
        return lax.rem(y + k + NY, NY)

    def remote(src, dst, ssem, rsem, device):
        return pltpu.make_async_remote_copy(
            src_ref=src, dst_ref=dst, send_sem=ssem, recv_sem=rsem, device_id=device, device_id_type=MESH
        )

    small = [
        pltpu.make_async_copy(src, dst, tsem.at[1 + i])
        for i, (src, dst) in enumerate(
            (
                (owner_in, owner),
                (slot_in, slot),
                (count_in, count),
                (entry_in, entry),
                (suffix_in, suffix),
                (decay_in, decay_log),
                (bias_in, step_bias),
                (skip_in, skip_gain),
            )
        )
    ]
    for copy in small:
        copy.start()

    barrier = pltpu.get_barrier_semaphore()
    peers = [(r, tp_of(d)) for d in range(1, NT)]
    peers += [(z_of(1) * NY + y, p), (z_of(-1) * NY + y, p)]
    peers += [(z * NY + y_of(j), p) for j in range(1, NY)]
    for peer in peers:
        pl.semaphore_signal(barrier, inc=1, device_id=peer, device_id_type=MESH)

    pending = []
    local = []

    def start(copy):
        copy.start()
        pending.append(copy)
        return copy

    def start_local(src, dst):
        copy = pltpu.make_async_copy(src, dst, lsem.at[len(local)])
        copy.start()
        local.append(copy)
        return copy

    my_rows = pl.ds(pl.multiple_of(p * ROWS, ROWS), ROWS)
    own_pool = start_local(pool, kz[0])

    pl.semaphore_wait(barrier, len(peers))

    def spread(i, src, dst, width):
        out = [start_local(src.at[:, pl.ds(pl.multiple_of(p * width, 128), width)], dst.at[my_rows, :])]
        for d in range(1, NT):
            to = tp_of(d)
            out.append(
                start(
                    remote(
                        src.at[:, pl.ds(pl.multiple_of(to * width, 128), width)],
                        dst.at[my_rows, :],
                        xs.at[i, d - 1],
                        xr.at[i, d - 1],
                        (r, to),
                    )
                )
            )
        return out

    def everyone(i, src, dst):
        out = [start_local(src, dst)]
        for d in range(1, NT):
            out.append(start(remote(src, dst, xs.at[i, d - 1], xr.at[i, d - 1], (r, tp_of(d)))))
        return out

    def arrive(copies):
        copies[0].wait()
        for copy in copies[1:]:
            copy.wait_recv()

    gathers = {}

    def gather_state(c):
        out = [start_local(state.at[c], yb[c].at[y])]
        for j in range(1, NY):
            out.append(
                start(
                    remote(
                        state.at[c],
                        yb[c].at[y],
                        sys_.at[c, j - 1],
                        syr.at[c, j - 1],
                        (z * NY + y_of(j), p),
                    )
                )
            )
        gathers[c] = out

    def length(parity, way):
        return 4 if (way > 0) == (parity == 0) else 3

    hops = {}

    def kv_slot(s, way):
        return DIST.index(s * way) if s < 4 else 7

    def kv_hop(f, s, way):
        slot_now = kv_slot(s, way)
        part = pl.ds(2 * f, 2)
        before = pool if s == 1 else kz[kv_slot(s - 1, way)]
        place = slot_now
        hops[f, s, way] = start(
            remote(
                before.at[part],
                kz[place].at[part],
                kzs.at[f, place],
                kzr.at[f, place],
                (z_of(way) * NY + y, p),
            )
        )

    kv_copies = {}

    def kv_across(k):
        source = lax.rem(z - DIST[k] + NZ, NZ) * NY + y
        for j in range(NY):
            to = y_of(j)
            word = tabs[source, to]
            first = kz[k][lax.rem(word, 4)]
            second = kz[k][lax.rem(lax.div(word, 4), 4)]
            if j == 0:
                kvb[k, y, 0] = first
                kvb[k, y, 1] = second
            else:
                ksend[k, j - 1, 0] = first
                ksend[k, j - 1, 1] = second
                kv_copies[k, j] = start(
                    remote(
                        ksend.at[k, j - 1],
                        kvb.at[k, y],
                        kys.at[k, j - 1],
                        kyr.at[k, j - 1],
                        (z * NY + to, p),
                    )
                )

    def kv_step(f, s):
        for way in (1, -1):
            if s <= length(f, way):
                hops[f, s, way].wait_recv()
                if s < length(f, way):
                    kv_hop(f, s + 1, way)
        if f == 1:
            if s < 4:
                kv_across(DIST.index(s))
                kv_across(DIST.index(-s))
            else:
                kv_across(7)

    tokens = {}

    def tok_hop(c, s, way):
        total = length(c % 2, way)
        dest = z_of(way * (total - s + 1))
        base = 0 if way > 0 else 4
        e = entry[dest * NY + y]
        mine = yb[c][lax.rem(e, NY)]
        if s > 1:
            mine = jnp.where(lax.div(e, NY) == z, mine, tk[c][base + s - 2])
        ts[c][base + s - 1] = mine
        tokens[c, s, way] = start(
            remote(
                ts[c].at[base + s - 1],
                tk[c].at[base + s - 1],
                tss.at[c, base + s - 1],
                tsr.at[c, base + s - 1],
                (z_of(way) * NY + y, p),
            )
        )

    def tok_start(c):
        arrive(gathers[c])
        tok_hop(c, 1, 1)
        tok_hop(c, 1, -1)

    def tok_step(c, s):
        for way in (1, -1):
            if s <= length(c % 2, way):
                tokens[c, s, way].wait_recv()
                if s < length(c % 2, way):
                    tok_hop(c, s + 1, way)

    for f in range(2):
        kv_hop(f, 1, 1)
        kv_hop(f, 1, -1)
    gather_state(0)
    gather_state(1)
    arrays = {}

    def leave(name):
        if name == "step":
            arrays[name] = everyone(0, step, stepb.at[my_rows, :])
        elif name == "proj":
            arrays[name] = spread(1, proj, projb, 512)
        elif name == "x":
            arrays[name] = spread(2, xin, xb, 1024)
        elif name == "q":
            arrays[name] = spread(3, query, qb, 512)
        elif name == "f":
            arrays[name] = spread(4, fresh, fb, 256)
        elif name == "gain":
            arrays[name] = everyone(5, gain, gainb.at[p])
        elif name == "gate":
            arrays[name] = start_local(gate, gateb)

    leave("step")

    for copy in small:
        copy.wait()
    lane = lax.broadcasted_iota(jnp.int32, (NZ * NY, 64), 1)
    who = lax.broadcasted_iota(jnp.int32, (NZ * NY, 64), 0)
    wide = lax.broadcasted_iota(jnp.int32, (NZ * NY, 128), 1)
    packed = jnp.zeros((NZ * NY, 128), jnp.int32)
    for t in range(NY):
        row = pl.ds(z * NY + t, 1)
        named = (owner[row, :] == who) & (lane < count[z * NY + t])
        code = lane * 4 + slot[row, :]
        first = jnp.min(jnp.where(named, code, 1024), axis=1, keepdims=True)
        last = jnp.max(jnp.where(named, code, -1), axis=1, keepdims=True)
        value = (
            (first & 3)
            + 4 * (last & 3)
            + jnp.where(first < 1024, 16, 0)
            + jnp.where(last > first, 32, 0)
        )
        packed = jnp.where(wide == t, value, packed)
    tabv[...] = packed
    to_scalars = pltpu.make_async_copy(tabv, tabs, tsem.at[0])
    to_scalars.start()

    to_scalars.wait()
    own_pool.wait()
    kv_across(0)
    live = suffix[r]

    side = lax.broadcasted_iota(jnp.int32, (1, 128), 1)

    lower = lax.broadcasted_iota(jnp.int32, (SPAN, SPAN), 0) >= lax.broadcasted_iota(
        jnp.int32, (SPAN, SPAN), 1
    )
    half = lax.broadcasted_iota(jnp.int32, (SPAN, 128), 1) < 64

    def scan_sums():
        arrive(arrays["step"])
        take = (
            lax.broadcasted_iota(jnp.int32, (128, 128), 0)
            == lax.broadcasted_iota(jnp.int32, (128, 128), 1) + p * 16
        ).astype(BF16)
        shift = jnp.zeros((1, 128), F32)
        rate = jnp.zeros((1, 128), F32)
        for h in range(16):
            shift = jnp.where(side == h, step_bias[h], shift)
            rate = jnp.where(side == h, decay_log[h], rate)
        raw = dot(stepb[...], take) + shift
        dt = jnp.maximum(raw, 0.0) + jnp.log1p(jnp.exp(-jnp.abs(raw)))
        drop = dt * -jnp.exp(rate)
        ones = lower.astype(F32)
        for b in range(2):
            rows = slice(b * SPAN, (b + 1) * SPAN)
            cum = dot(ones, drop[rows], precision=lax.Precision.HIGHEST)
            cum_c[rows, :] = cum
            cum_r[b] = cum.T
            dt_r[b] = dt[rows].T
            if b == 0:
                w_c[...] = jnp.exp(cum[SPAN - 1 : SPAN] - cum) * dt[rows]

    def scan_inner():
        arrive(arrays["proj"])
        for b in range(2):
            rows = slice(b * SPAN, (b + 1) * SPAN)
            inner[b] = dot(projb[rows, 256:512], projb[rows, 0:256], BT)
        arrive(arrays["x"])

    def pair(hp, carry):
        cols = pl.ds(pl.multiple_of(hp * 128, 128), 128)
        skip = jnp.where(half, skip_gain[hp * 2], skip_gain[hp * 2 + 1])
        for b in range(2):
            rows = slice(b * SPAN, (b + 1) * SPAN)
            xp = xb[rows, cols]
            cum_b = cum_c[rows, :]
            res, cumcols, weights = [], [], []
            for e in range(2):
                h = hp * 2 + e
                column = pltpu.roll(cum_b, 128 - h, 1)[:, 0:1]
                spread_cum = column - cum_r[b, pl.ds(h, 1), :]
                mix = jnp.exp(jnp.where(lower, spread_cum, LOW)) * inner[b] * dt_r[b, pl.ds(h, 1), :]
                res.append(dot(mix.astype(BF16), xp))
                cumcols.append(column)
                if b == 0:
                    weights.append(pltpu.roll(w_c[...], 128 - h, 1)[:, 0:1])
            xf = xp.astype(F32)
            ecx[rows, cols] = jnp.exp(jnp.where(half, cumcols[0], cumcols[1]))
            yint[rows, cols] = jnp.where(half, res[0], res[1]) + skip * xf
            if b == 0:
                tailb[:, cols] = (jnp.where(half, weights[0], weights[1]) * xf).astype(BF16)
        return carry

    def scan_add():
        add_s[...] = dot(projb[0:SPAN, 0:256], tailb[...], AT)

    def open_gate():
        arrays["gate"].wait()

        def some(g, carry):
            cols = pl.ds(pl.multiple_of(g * 1024, 1024), 1024)
            gv = gateb[:, cols].astype(F32)
            gact[:, cols] = gv / (1.0 + jnp.exp(-gv))
            return carry

        lax.fori_loop(0, NT, some, 0)

    ssm_sends = []

    def carry_in(lo, hi):
        e = entry[r]
        ze = lax.div(e, NY)
        behind = lax.rem(z - ze + NZ, NZ)
        eye = (
            lax.broadcasted_iota(jnp.int32, (256, 256), 0) == lax.broadcasted_iota(jnp.int32, (256, 256), 1)
        ).astype(BF16)
        for c in range(lo, hi):
            ahead, back = length(c % 2, 1), length(c % 2, -1)
            entering = jnp.where(behind <= ahead, tk[c][ahead - 1], tk[c][4 + back - 1])
            s0 = jnp.where(ze == z, yb[c][lax.rem(e, NY)], entering)
            cols = slice(c * 128, (c + 1) * 128)
            s0t = dot(eye, s0, BT)
            s1t = ecx[SPAN - 1 : SPAN, cols] * s0t + add_s[:, cols]
            for b, st in ((0, s0t), (1, s1t)):
                rows = slice(b * SPAN, (b + 1) * SPAN)
                carried = dot(projb[rows, 256:512], st.astype(BF16))
                osend[rows, cols] = (yint[rows, cols] + ecx[rows, cols] * carried).astype(BF16)
        cols = slice(lo * 128, hi * 128)
        for d in range(1, NT):
            to = tp_of(d)
            ssm_sends.append(
                start(
                    remote(
                        osend.at[pl.ds(pl.multiple_of(to * ROWS, ROWS), ROWS), cols],
                        ob.at[my_rows, cols],
                        oss.at[lo, d - 1],
                        osr.at[lo, d - 1],
                        (r, to),
                    )
                )
            )
        ob[my_rows, cols] = osend[my_rows, cols]

    def set_block(block, rows):
        kk[0:rows, 0:128] = block[:, 0:128]
        kk[0:rows, 128:256] = block[:, 0:128]
        vt[0:128, 0:rows] = block[:, 128:256].T

    def attend_first():
        arrive(arrays["q"])
        arrive(arrays["f"])
        for head in range(4):
            qf = qb[:, head * 128 : (head + 1) * 128].astype(F32) * SCALE
            high = qf.astype(BF16)
            q2[head, :, 0:128] = high
            q2[head, :, 128:256] = (qf - high.astype(F32)).astype(BF16)
        vt[128:144, :] = jnp.ones((16, 1024), BF16)
        set_block(fb[...], 512)
        allowed = lax.broadcasted_iota(jnp.int32, (512, 512), 0) <= lax.broadcasted_iota(
            jnp.int32, (512, 512), 1
        )
        for head in range(4):
            s = jnp.where(allowed, dot(kk[0:512, :], q2[head], BT), LOW)
            top = jnp.max(s, axis=0, keepdims=True)
            w = jnp.exp2(s - top).astype(BF16)
            m_s[head] = jnp.broadcast_to(top, (8, 512))
            acc_s[head] = dot(vt[:, 0:512], w)

    def attend_cached(n, part):
        if part == 0:
            for k in (2 * n, 2 * n + 1):
                for j in range(1, NY):
                    kv_copies[k, j].wait_recv()
            set_block(kvb[2 * n : 2 * n + 2].reshape(1024, 256), 1024)
        blocked = []
        for k in (2 * n, 2 * n + 1):
            for t in range(NY):
                word = tabs[lax.rem(z - DIST[k] + NZ, NZ) * NY + t, y]
                blocked.append(jnp.where(lax.rem(lax.div(word, 16), 2) > 0, 0.0, LOW))
                blocked.append(jnp.where(lax.div(word, 32) > 0, 0.0, LOW))
        for head in (2 * part, 2 * part + 1):
            s = dot(kk[...], q2[head], BT)
            s = jnp.concatenate([s[b * 64 : (b + 1) * 64] + blocked[b] for b in range(16)], axis=0)
            old = m_s[head][0:1, :]
            top = jnp.maximum(old, jnp.max(s, axis=0, keepdims=True))
            w = jnp.exp2(s - top).astype(BF16)
            m_s[head] = jnp.broadcast_to(top, (8, 512))
            acc_s[head] = acc_s[head] * jnp.exp2(old - top) + dot(vt[...], w)

    my_cols = pl.ds(pl.multiple_of(p * 512, 512), 512)
    attn_sends = []
    own_attn = []

    def attend_last():
        alive = lax.broadcasted_iota(jnp.int32, (128, 512), 1) < live
        for head in range(4):
            value = jnp.where(alive, acc_s[head, 0:128] / acc_s[head, 128:129], 0.0)
            ao[:, head * 128 : (head + 1) * 128] = value.T.astype(BF16)
        for d in range(1, NT):
            to = tp_of(d)
            attn_sends.append(
                start(
                    remote(
                        ao.at[pl.ds(pl.multiple_of(to * ROWS, ROWS), ROWS), :],
                        attn_out.at[:, my_cols],
                        aos.at[d - 1],
                        aor.at[d - 1],
                        (r, to),
                    )
                )
            )
        own_attn.append(start_local(ao.at[my_rows, :], attn_out.at[:, my_cols]))

    waiting = [("kv", 0), ("kv", 1)] + [("st", c) for c in range(PARTS)]
    under_way = []
    ended = []
    work = list(WORK)
    done = set()
    count_rounds = 0
    marks = []

    def do(item):
        name, args = item[1], item[2:]
        if name == "sums":
            scan_sums()
        elif name == "inner":
            scan_inner()
        elif name == "pair":
            lax.fori_loop(args[0], args[1], pair, 0)
        elif name == "carry":
            carry_in(*args)
        elif name == "fresh":
            attend_first()
        elif name == "cached":
            attend_cached(*args)
        elif name == "finish":
            attend_last()
        elif name == "leave":
            leave(*args)
        elif name == "gather":
            for c in range(*args):
                gather_state(c)
        elif name == "add":
            scan_add()
        elif name == "gate":
            open_gate()
        elif name == "gain":
            arrive(arrays["gain"])
        elif name == "drain":
            while pending[0] is not marks[args[0]]:
                pending.pop(0).wait_send()

    def able(item):
        if item[1] == "carry":
            return all(c in done for c in range(item[2], item[3]))
        return item[0] <= count_rounds

    while waiting or under_way:
        for one in list(under_way):
            kind, n, s = one
            (kv_step if kind == "kv" else tok_step)(n, s)
            if s == 4:
                under_way.remove(one)
                if kind == "st":
                    done.add(n)
            else:
                under_way[under_way.index(one)] = (kind, n, s + 1)
        room = 2 if count_rounds < 1 else 1
        while waiting and len(under_way) < FLIGHT and room > 0:
            room -= 1
            kind, n = waiting.pop(0)
            if kind == "st":
                tok_start(n)
            under_way.append((kind, n, 1))
        count_rounds += 1
        marks.append(pending[-1])
        budget = BUDGET
        for item in list(work):
            if budget > 0 and able(item):
                work.remove(item)
                do(item)
                budget -= COST[item[1]]
    for item in list(work):
        do(item)

    own_attn[0].wait()
    for copy in attn_sends:
        copy.wait_recv()
    for copy in pending:
        copy.wait_send()
    for copy in ssm_sends:
        copy.wait_recv()

    def norm(g, carry):
        rows = pl.ds(pl.multiple_of(g * ROWS, ROWS), ROWS)
        parts = []
        square = jnp.zeros((ROWS, 1), F32)
        for c in range(4):
            act = gact[:, pl.ds(pl.multiple_of(g * 1024 + c * 256, 256), 256)]
            gated = ob[rows, c * 256 : (c + 1) * 256].astype(F32) * act
            parts.append(gated)
            square = square + jnp.sum(gated * gated, axis=1, keepdims=True)
        factor = lax.rsqrt(square * (1.0 / 1024) + 1e-5)
        alive = lax.broadcasted_iota(jnp.int32, (ROWS, 1), 0) + p * ROWS < live
        factor = jnp.where(alive, factor, 0.0)
        gains = gainb[g]
        for c in range(4):
            for e in range(2):
                k = c * 2 + e
                ssm_out[:, pl.ds(pl.multiple_of(g * 1024 + k * 128, 128), 128)] = (
                    parts[c][:, e * 128 : (e + 1) * 128] * factor * gains[k : k + 1, :]
                ).astype(BF16)
        return carry

    lax.fori_loop(0, NT, norm, 0)


BUDGET = 4.5
COST = {
    "leave": 0.5,
    "gather": 0.4,
    "sums": 1.0,
    "inner": 0.5,
    "pair": 1.5,
    "add": 0.6,
    "carry": 1.2,
    "fresh": 2.5,
    "cached": 2.0,
    "finish": 1.0,
    "gate": 1.2,
    "gain": 0.1,
    "drain": 0.3,
}
WORK = (
    (1, "leave", "proj"),
    (1, "leave", "x"),
    (1, "gather", 2, 4),
    (2, "gather", 4, 6),
    (2, "leave", "q"),
    (2, "leave", "f"),
    (3, "gather", 6, 8),
    (3, "leave", "gain"),
    (3, "leave", "gate"),
    (3, "sums"),
    (4, "gate"),
    (4, "inner"),
    (4, "pair", 0, 2),
    (4, "pair", 2, 4),
    (5, "pair", 4, 6),
    (5, "pair", 6, 8),
    (5, "add"),
    (6, "carry", 0, 2),
    (6, "gain"),
    (6, "fresh"),
    (6, "carry", 2, 4),
    (7, "drain", 1),
    (7, "cached", 0, 0),
    (7, "cached", 0, 1),
    (8, "carry", 4, 6),
    (8, "cached", 1, 0),
    (8, "cached", 1, 1),
    (9, "drain", 4),
    (9, "cached", 2, 0),
    (9, "cached", 2, 1),
    (10, "cached", 3, 0),
    (10, "cached", 3, 1),
    (10, "finish"),
    (11, "drain", 8),
    (12, "carry", 6, 7),
    (12, "carry", 7, 8),
)


def run(*args):
    any_ = pl.BlockSpec(memory_space=pl.ANY)
    vmem = pl.BlockSpec(memory_space=pltpu.VMEM)
    dma = pltpu.SemaphoreType.DMA
    return pl.pallas_call(
        kernel,
        out_shape=(
            jax.ShapeDtypeStruct((ROWS, 8192), BF16),
            jax.ShapeDtypeStruct((ROWS, 4096), BF16),
        ),
        in_specs=[any_] * 17,
        out_specs=(vmem, any_),
        scratch_shapes=[
            pltpu.VMEM((NZ * NY, 64), jnp.int32),
            pltpu.VMEM((NZ * NY, 64), jnp.int32),
            pltpu.SMEM((NZ * NY,), jnp.int32),
            pltpu.SMEM((NZ * NY,), jnp.int32),
            pltpu.SMEM((NZ * NY,), jnp.int32),
            pltpu.SMEM((16,), F32),
            pltpu.SMEM((16,), F32),
            pltpu.SMEM((16,), F32),
            pltpu.VMEM((NZ * NY, 128), jnp.int32),
            pltpu.SMEM((NZ * NY, 128), jnp.int32),
            pltpu.VMEM((512, 128), BF16),
            pltpu.VMEM((NT, 8, 128), F32),
            pltpu.VMEM((512, 512), BF16),
            pltpu.VMEM((512, 1024), BF16),
            pltpu.VMEM((512, 512), BF16),
            pltpu.VMEM((512, 256), BF16),
            pltpu.VMEM((ROWS, 8192), BF16),
            pltpu.VMEM((ROWS, 8192), F32),
            pltpu.VMEM((256, 1024), F32),
            [pltpu.VMEM((4, 64, 256), BF16)] * 8,
            pltpu.VMEM((8, 3, 2, 64, 256), BF16),
            pltpu.VMEM((8, NY, 2, 64, 256), BF16),
            [pltpu.VMEM((NY, 128, 256), BF16)] * PARTS,
            [pltpu.VMEM((8, 128, 256), BF16)] * PARTS,
            [pltpu.VMEM((8, 128, 256), BF16)] * PARTS,
            pltpu.VMEM((512, 128), F32),
            pltpu.VMEM((256, 128), F32),
            pltpu.VMEM((2, 128, 256), F32),
            pltpu.VMEM((2, 128, 256), F32),
            pltpu.VMEM((2, 256, 256), F32),
            pltpu.VMEM((512, 1024), F32),
            pltpu.VMEM((512, 1024), F32),
            pltpu.VMEM((256, 1024), BF16),
            pltpu.VMEM((512, 1024), BF16),
            pltpu.VMEM((512, 1024), BF16),
            pltpu.VMEM((4, 512, 256), BF16),
            pltpu.VMEM((1024, 256), BF16),
            pltpu.VMEM((144, 1024), BF16),
            pltpu.VMEM((4, 8, 512), F32),
            pltpu.VMEM((4, 144, 512), F32),
            pltpu.VMEM((512, 512), BF16),
            dma((9,)),
            dma((24,)),
            dma((6, 7)),
            dma((6, 7)),
            dma((2, 8)),
            dma((2, 8)),
            dma((8, 3)),
            dma((8, 3)),
            dma((PARTS, 3)),
            dma((PARTS, 3)),
            dma((PARTS, 8)),
            dma((PARTS, 8)),
            dma((PARTS, 7)),
            dma((PARTS, 7)),
            dma((7,)),
            dma((7,)),
        ],
        compiler_params=pltpu.CompilerParams(
            collective_id=0, has_side_effects=True, vmem_limit_bytes=56 * 2**20
        ),
        name="prefill",
    )(*args)


def per_device(
    ssm_input,
    ssm_gate,
    state_proj,
    step_raw,
    queries,
    fresh_kv,
    block_pool,
    state_pool,
    decay_log,
    step_bias,
    skip_gain,
    norm_gain,
    block_owner,
    block_slot,
    block_count,
    state_entry,
    suffix_len,
):
    ssm, attn = run(
        block_owner,
        block_slot,
        block_count,
        state_entry,
        suffix_len,
        decay_log,
        step_bias,
        skip_gain,
        norm_gain.reshape(8, 128),
        step_raw[0],
        state_proj[0],
        ssm_input[0],
        queries[0],
        fresh_kv[0],
        ssm_gate[0],
        block_pool.reshape(4, 64, 256),
        state_pool.reshape(PARTS, 128, 256),
    )
    return (ssm[None], attn[None])


def solution(mesh):
    return jax.shard_map(
        per_device,
        mesh=mesh,
        in_specs=(
            P("req", "tp", None),
            P("req", "tp", None),
            P("req", "tp", None),
            P("req", "tp", None),
            P("req", "tp", None),
            P("req", "tp", None),
            P("req", None, "tp", None),
            P("req", "tp", None, None),
            P("tp"),
            P("tp"),
            P("tp"),
            P("tp"),
            P(),
            P(),
            P(),
            P(),
            P(),
        ),
        out_specs=(P("req", "tp", None), P("req", "tp", None)),
        check_vma=False,
    )
```
